512 devices in a mesh: ctx: 64 (over z_hi, y, core), kvh: 8 (over x, z_lo).
Axes of the slice: x: 4, y: 8, z: 8 (z_hi: 4, z_lo: 2; z = z_hi * 2 + z_lo), core: 2. Of those that a mesh axis runs over, the one named last changes fastest.
Arguments:
- queries: bfloat16 [24576, 64, 128], P(('ctx', 'kvh')), may hold values from -160 to 160
- keys: bfloat16 [24576, 8, 128], P(('ctx', 'kvh')), may hold values from -6 to 6
- values: bfloat16 [24576, 8, 128], P(('ctx', 'kvh')), may hold values from -6 to 6
- grad_out: bfloat16 [24576, 64, 128], P(('ctx', 'kvh')), may hold values from -6 to 6
- segment_ids: int32 [24576], replicated, may hold values from 0 to 63, never falling along the last dimension, each value on 1 to 1152 neighbouring positions
Outputs:
- attention: bfloat16 [24576, 64, 128], P('ctx', 'kvh')
- grad_queries: bfloat16 [24576, 64, 128], P('ctx', 'kvh')
- grad_keys: bfloat16 [24576, 8, 128], P('ctx', 'kvh')
- grad_values: bfloat16 [24576, 8, 128], P('ctx', 'kvh')
The draws below stay inside these ranges and needn't reach their ends.
Inputs may be any that keep to these rules, and one draw needn't show every extreme that they name: `segment_ids`: Non-decreasing from 0 without gaps; every document has 1 to 1152 positions, and one has exactly that many.
All inputs are finite; a program needn't handle non-finite values.
Results may differ from the reference program's by a relative error of at most 0.013.
Values may be sent and summed in bfloat16 or wider, within the bound.
A program may use at most 64 MiB of HBM per device.

```python
import math
import jax
import jax.numpy as jnp
import numpy as np
from jax import lax

HEAD_DIM = 128
KV_HEADS = 8
QPK = 8
TOK_DEV = 384
SPAN = 3
HEADS = 64
TOKENS = 24576
N_CTX = 64


def shared_parts(key):
    key_base = jnp.clip(jax.random.normal(jax.random.fold_in(key, 101), (TOKENS, KV_HEADS, HEAD_DIM), jnp.float32), -5.0, 5.0)
    return key_base


def draw_keys(key, part):
    key_base = shared_parts(key)
    return key_base.astype(jnp.bfloat16)


def draw_queries(key, part):
    key = jax.random.fold_in(key, 2)
    query_base = jnp.clip(jax.random.normal(key, (TOKENS, HEADS, HEAD_DIM), jnp.float32), -5.0, 5.0)
    return query_base.astype(jnp.bfloat16)


def shard_levels(own_key, extent, split, low, largest):
    factor_of = 1.0
    for dim, parts in split:
        draws = jax.random.uniform(jax.random.fold_in(jax.random.fold_in(own_key, 6), dim), (parts,), jnp.float32, low / len(split), largest / len(split))
        factor_of = factor_of * jnp.repeat(jnp.exp(draws), extent[dim] // parts).reshape((-1,) + (1,) * (len(extent) - 1 - dim))
    return factor_of


def length_profile(count, total, reach, lean):
    loads = [(1 << 20) // math.isqrt(rank ** lean) + 1 for rank in range(2, count + 1)]
    surplus, counts = total - reach - (count - 1), [1] * (count - 1)
    while surplus > 0:
        free = [i for i in range(count - 1) if counts[i] < reach]
        mass, left = sum([loads[i] for i in free]), surplus
        for i in free:
            addition = min(reach - counts[i], max(1, left * loads[i] // mass), surplus)
            counts[i] = counts[i] + addition
            surplus = surplus - addition
    return np.array([reach] + counts)


def uneven_parts(key, count, total, limit, skew):
    if count == 2:
        one = jax.random.randint(key, (), max(1, total - limit), min(limit, total - 1) + 1)
        return jnp.stack([one, total - one])
    tallies = jnp.asarray(length_profile(count, total, limit, skew), jnp.int32)
    pairs = (count - 1) // 2
    donor, receiver = tallies[1:1 + 2 * pairs:2], tallies[2:2 + 2 * pairs:2]
    slack = jnp.minimum(donor - 1, limit - receiver)
    moved = jax.random.randint(jax.random.fold_in(key, 1), (pairs,), 0, 1 << 20) % (slack + 1)
    tallies = tallies.at[1:1 + 2 * pairs:2].set(donor - moved).at[2:2 + 2 * pairs:2].set(receiver + moved)
    return tallies[jax.random.permutation(jax.random.fold_in(key, 2), count)]


def gaussian(key, dims, deviation, bound, cuts=(), kind=jnp.bfloat16):
    loudness = shard_levels(key, dims, cuts, -0.22, 0.18) if cuts else 1.0
    entries = jax.random.normal(key, dims, jnp.float32) * deviation * loudness
    return jnp.minimum(jnp.maximum(entries, -bound), bound).astype(kind)


def setup_inputs(seed: int = 0) -> dict:
    streams_of = jax.random.split(jax.random.key(seed), 6)
    return {
        "queries": draw_queries(jax.random.fold_in(streams_of[5], 71), 0),
        "keys": draw_keys(jax.random.fold_in(streams_of[5], 71), 0),
        "values": gaussian(streams_of[2], (TOKENS, KV_HEADS, HEAD_DIM), 1.0, 6.0, ((0, 512),)),
        "grad_out": gaussian(streams_of[3], (TOKENS, HEADS, HEAD_DIM), 1.0, 6.0, ((0, 512),)),
        "segment_ids": jnp.searchsorted(jnp.cumsum(uneven_parts(streams_of[4], TOKENS // TOK_DEV, TOKENS, SPAN * TOK_DEV, 2)), jnp.arange(TOKENS), side="right").astype(jnp.int32),
    }


def reference(queries, keys, values, grad_out, segment_ids):
    score_scale = 1.0 / math.sqrt(HEAD_DIM)
    front_pad = SPAN * TOK_DEV
    window = front_pad + TOK_DEV
    keys_padded = jnp.concatenate([jnp.zeros((front_pad, KV_HEADS, HEAD_DIM), keys.dtype), keys], axis=0)
    values_padded = jnp.concatenate([jnp.zeros((front_pad, KV_HEADS, HEAD_DIM), values.dtype), values], axis=0)
    segments_padded = jnp.concatenate([jnp.full((front_pad,), -1, jnp.int32), segment_ids.astype(jnp.int32)])
    query_blocks = queries.reshape(N_CTX, TOK_DEV, KV_HEADS, QPK, HEAD_DIM)
    grad_blocks = grad_out.reshape(N_CTX, TOK_DEV, KV_HEADS, QPK, HEAD_DIM)

    def block_step(running, inputs):
        key_sums, value_sums = running
        block_index, query_block, grad_block = inputs
        row_start = (block_index * TOK_DEV).astype(jnp.int32)
        key_wide = lax.dynamic_slice_in_dim(keys_padded, row_start, window, 0).astype(jnp.float32)
        value_wide = lax.dynamic_slice_in_dim(values_padded, row_start, window, 0).astype(jnp.float32)
        key_segments = lax.dynamic_slice_in_dim(segments_padded, row_start, window, 0)
        query_segments = lax.dynamic_slice_in_dim(segment_ids.astype(jnp.int32), row_start, TOK_DEV, 0)
        query_places = row_start + jnp.arange(TOK_DEV, dtype=jnp.int32)
        key_places = row_start - front_pad + jnp.arange(window, dtype=jnp.int32)
        allowed = (query_segments[:, None] == key_segments[None, :]) & (key_places[None, :] <= query_places[:, None])
        query_wide = query_block.astype(jnp.float32)
        grad_wide = grad_block.astype(jnp.float32)
        scores = jnp.einsum('bgqd,wgd->gqbw', query_wide, key_wide) * score_scale
        scores = jnp.where(allowed, scores, -1e+30)
        highest = lax.optimization_barrier(jnp.max(scores, axis=-1, keepdims=True))
        log_total = highest + jnp.log(lax.optimization_barrier(jnp.sum(jnp.exp(scores - highest), axis=-1, keepdims=True)))
        probs_full = jnp.exp(scores - log_total)
        probs_low = lax.optimization_barrier(probs_full.astype(jnp.bfloat16))
        attended = jnp.einsum('gqbw,wgd->bgqd', probs_low.astype(jnp.float32), value_wide).astype(jnp.bfloat16)
        attended = lax.optimization_barrier(attended)
        grad_probs = jnp.einsum('bgqd,wgd->gqbw', grad_wide, value_wide)
        deltas = lax.optimization_barrier(jnp.sum(grad_wide * attended.astype(jnp.float32), axis=-1)).transpose(1, 2, 0)[..., None]
        grad_scores = (probs_full * (grad_probs - deltas) * score_scale).astype(jnp.bfloat16)
        grad_scores = lax.optimization_barrier(grad_scores)
        grad_query = jnp.einsum('gqbw,wgd->bgqd', grad_scores.astype(jnp.float32), key_wide).astype(jnp.bfloat16)
        grad_key = jnp.einsum('gqbw,bgqd->wgd', grad_scores.astype(jnp.float32), query_wide)
        grad_value = jnp.einsum('gqbw,bgqd->wgd', probs_low.astype(jnp.float32), grad_wide)
        key_sums = lax.dynamic_update_slice_in_dim(key_sums, lax.dynamic_slice_in_dim(key_sums, row_start, window, 0) + grad_key, row_start, 0)
        value_sums = lax.dynamic_update_slice_in_dim(value_sums, lax.dynamic_slice_in_dim(value_sums, row_start, window, 0) + grad_value, row_start, 0)
        return ((key_sums, value_sums), (attended, grad_query))
    zero_sums = jnp.zeros((front_pad + TOKENS, KV_HEADS, HEAD_DIM), jnp.float32)
    (key_sums, value_sums), (attended_all, grad_all) = lax.scan(block_step, (zero_sums, zero_sums), (jnp.arange(N_CTX, dtype=jnp.int32), query_blocks, grad_blocks))
    attention = attended_all.reshape(TOKENS, HEADS, HEAD_DIM)
    grad_queries = grad_all.reshape(TOKENS, HEADS, HEAD_DIM)
    grad_keys = key_sums[front_pad:].astype(jnp.bfloat16)
    grad_values = value_sums[front_pad:].astype(jnp.bfloat16)
    return (attention, grad_queries, grad_keys, grad_values)
```

```python
import functools
import math

import jax
import jax.numpy as jnp
from jax import lax
from jax.experimental import pallas as pl
from jax.experimental.pallas import tpu as pltpu
from jax.sharding import PartitionSpec as P

MESH = pl.DeviceIdType.MESH
SPAN = 3
BIG = 1e30
F32 = jnp.float32
BF16 = jnp.bfloat16

ROWS = 384
PIECE = 48
GROUPS = 8
QPK = 8
DIM = 128
PAIR = 2 * PIECE
PAIRS = ROWS // PAIR
COLS = PAIR * QPK
WINDOW = (SPAN + 1) * ROWS
BAND = SPAN * ROWS + PAIR
SCALE = 1.0 / math.sqrt(DIM)
LOG2E = math.log2(math.e)

NT = (((1,), (1,)), ((), ()))
TN = (((0,), (0,)), ((), ()))
NN = (((1,), (0,)), ((), ()))


def dot(a, b, dims):
    return lax.dot_general(a, b, dims, preferred_element_type=F32)


def kernel(
    n_ctx,
    q_ref, do_ref, k_ref, v_ref, seg_ref,
    att_ref, dq_ref, dk_ref, dv_ref,
    stage, kvsend, kvwin, ohk, ohq, qbuf, dobuf, qm, dom, doms, s_ref, p_all, delta, rls,
    dqt, dk_acc, dv_acc, gsend, grecv,
    a2a_send, a2a_recv, fwd_send, fwd_recv, g_send, g_recv,
):
    c = lax.axis_index("ctx")
    g = lax.axis_index("kvh")
    x = g // 2
    odd = lax.rem(c, 2)
    sibling = c + 1 - 2 * odd

    def along(steps):
        return lax.rem(c + (steps + n_ctx), n_ctx)

    barrier = pltpu.get_barrier_semaphore()
    for s in range(1, GROUPS):
        pl.semaphore_signal(
            barrier, inc=1, device_id=(c, lax.rem(g + s, GROUPS)), device_id_type=MESH
        )
    for steps in (1, -1, 2, -2):
        pl.semaphore_signal(barrier, inc=1, device_id=(along(steps), g), device_id_type=MESH)

    for i, ref in enumerate((k_ref, v_ref)):
        stage[...] = ref[...].astype(F32).reshape(PIECE * GROUPS, DIM)
        for h in range(GROUPS):
            kvsend[h, i] = stage[pl.ds(h, PIECE, stride=GROUPS), :].astype(BF16)

    pl.semaphore_wait(barrier, GROUPS - 1 + 4)

    own = SPAN * ROWS
    my_rows = pl.ds(pl.multiple_of(g * PIECE, PIECE), PIECE)

    def kv_slot(i):
        return kvwin.at[i, pl.ds(pl.multiple_of(own + g * PIECE, PIECE), PIECE)]

    def kv_copy(i, peer, slot):
        return pltpu.make_async_remote_copy(
            src_ref=kvsend.at[peer, i], dst_ref=kv_slot(i),
            send_sem=a2a_send.at[i, slot], recv_sem=a2a_recv.at[i, g],
            device_id=(c, peer), device_id_type=MESH,
        )

    def wide_copy(i, src, dst, peer, slot):
        return pltpu.make_async_remote_copy(
            src_ref=src.at[:, peer], dst_ref=dst.at[my_rows],
            send_sem=a2a_send.at[i, slot], recv_sem=a2a_recv.at[i, g],
            device_id=(c, peer), device_id_type=MESH,
        )

    peers = []
    z = lax.rem(g, 2)
    for step in (0, 1, 3, 2):
        px = lax.rem(x + step, PAIRS)
        for other in (0, 1):
            if step == 0 and other == 0:
                continue
            peers.append(2 * px + lax.rem(z + other, 2))

    for i in range(2):
        for slot, peer in enumerate(peers):
            kv_copy(i, peer, slot).start()
        pltpu.make_async_copy(kvsend.at[g, i], kv_slot(i), a2a_recv.at[i, g]).start()
    pltpu.make_async_copy(q_ref.at[:, g], qbuf.at[my_rows], a2a_recv.at[2, g]).start()
    pltpu.make_async_copy(do_ref.at[:, g], dobuf.at[my_rows], a2a_recv.at[3, g]).start()
    for slot, peer in enumerate(peers):
        wide_copy(2, q_ref, qbuf, peer, slot).start()
        wide_copy(3, do_ref, dobuf, peer, slot).start()

    def arrived(ref, sem):
        pltpu.make_async_copy(ref, ref, sem).wait()

    tiles = WINDOW // DIM
    seg_rows = n_ctx * ROWS // DIM
    first = c * (ROWS // DIM) + seg_rows - SPAN * (ROWS // DIM)
    number = lax.broadcasted_iota(jnp.int32, (DIM, DIM), 0)
    for i in range(tiles):
        row = seg_ref[pl.ds(lax.rem(first + i, seg_rows), 1), :]
        hot = jnp.where(number == row, 1.0, 0.0).T
        ohk[i * DIM : (i + 1) * DIM, :] = hot.astype(BF16)
        if i >= tiles - ROWS // DIM:
            at = (i - (tiles - ROWS // DIM)) * DIM
            ohq[at : at + DIM, :] = (hot - 1.0) * BIG
    dk_acc[...] = jnp.zeros_like(dk_acc)
    dv_acc[...] = jnp.zeros_like(dv_acc)
    dqt[...] = jnp.zeros_like(dqt)

    def block(i, d):
        return kvwin.at[i, pl.ds(own - d * ROWS, ROWS)]

    def fwd_copy(i, n, src, d, there):
        return pltpu.make_async_remote_copy(
            src_ref=src, dst_ref=block(i, d),
            send_sem=fwd_send.at[i, n], recv_sem=fwd_recv.at[i, d - 1],
            device_id=(there, g), device_id_type=MESH,
        )

    def to_two(i):
        return fwd_copy(i, 0, block(i, 0), 2, along(2))

    def to_sibling(i, d):
        return fwd_copy(i, 1, block(i, d), 1, sibling)

    def to_three(i):
        return fwd_copy(i, 2, block(i, 2), 3, along(1))

    for i in range(2):
        for j in range(GROUPS):
            arrived(kvwin.at[i, pl.ds(own + j * PIECE, PIECE)], a2a_recv.at[i, j])
        to_two(i).start()

        @pl.when(odd == 0)
        def _():
            to_sibling(i, 0).start()

    for i in range(2):
        arrived(block(i, 2), fwd_recv.at[i, 1])
        to_three(i).start()

        @pl.when(odd == 1)
        def _():
            to_sibling(i, 2).start()

    for d in (1, 3):
        arrived(block(0, d), fwd_recv.at[0, d - 1])

    def forward(t, carry):
        step = jnp.where(t == 0, 0, jnp.where(t == 1, 3, jnp.where(t == 2, 1, 2)))
        jj = lax.rem(x + step, PAIRS)
        base = pl.multiple_of(jj * PAIR, PAIR)
        rows = pl.ds(base, PAIR)
        for half in range(2):
            piece = pl.ds(pl.multiple_of(base + half * PIECE, PIECE), PIECE)
            arrived(qbuf.at[piece], a2a_recv.at[2, 2 * jj + half])
            arrived(dobuf.at[piece], a2a_recv.at[3, 2 * jj + half])
        qf = qbuf[rows].astype(F32).reshape(COLS, DIM)
        qb = qf.astype(BF16)
        penalty = jnp.broadcast_to(ohq[rows, :][:, None, :], (PAIR, QPK, DIM))
        qa = jnp.concatenate([qb, penalty.reshape(COLS, DIM).astype(BF16)], axis=1)
        part = BAND // 3
        m8 = None
        for ch in range(3):
            keys = pl.ds(pl.multiple_of(base + ch * part, 32), part)
            ka = jnp.concatenate([kvwin[0, keys, :], ohk[keys, :]], axis=1)
            s = dot(ka, qa, NT)
            if ch == 2:
                tail = s[part - PAIR :]
                key_at = lax.broadcasted_iota(jnp.int32, (PAIR, COLS), 0) * QPK
                col_at = lax.broadcasted_iota(jnp.int32, (PAIR, COLS), 1)
                tail = jnp.where(key_at <= col_at, tail, -BIG)
                s = jnp.concatenate([s[: part - PAIR], tail], axis=0)
            s_ref[ch * part : (ch + 1) * part, :] = s
            top = jnp.max(s.reshape(part // 8, 8, COLS), axis=0)
            m8 = top if m8 is None else jnp.maximum(m8, top)
        m = jnp.max(m8, axis=0, keepdims=True)
        l8 = jnp.zeros((8, COLS), F32)
        for ch in range(BAND // PAIR):
            at = slice(ch * PAIR, (ch + 1) * PAIR)
            e = jnp.exp2((s_ref[at, :] - m) * (SCALE * LOG2E))
            l8 = l8 + jnp.sum(e.reshape(PAIR // 8, 8, COLS), axis=0)
            p_all[jj, at, :] = e.astype(BF16)
        rl = 1.0 / jnp.sum(l8, axis=0, keepdims=True)
        rls[jj] = rl
        by_row = jnp.broadcast_to(rl, (DIM, COLS)).T
        qm[jj] = (qf * by_row).astype(BF16)
        dof = dobuf[rows].astype(F32).reshape(COLS, DIM)
        dom[jj] = dof.astype(BF16)
        doms[jj] = (dof * by_row).astype(BF16)

        @pl.when(t == 0)
        def _():
            for d in (1, 3):
                arrived(block(1, d), fwd_recv.at[1, d - 1])

        band = pl.ds(base, BAND)
        ot = dot(kvwin[1, band, :], p_all[jj], TN) * rl
        ot = ot.astype(BF16).astype(F32)
        att_ref[rows] = ot.T.reshape(PAIR, QPK, DIM).astype(BF16)
        delta[jj] = jnp.sum(dof.T * ot, axis=0, keepdims=True)
        return carry

    lax.fori_loop(0, PAIRS, forward, 0)

    def unit(jj, key_lo, size, off):
        keys = slice(key_lo, key_lo + size)
        ks = kvwin[0, keys, :]
        p = p_all[jj, pl.ds(off, size), :]
        dpt = dot(kvwin[1, keys, :], dom[jj], NT)
        ds = p * (dpt - delta[jj]).astype(BF16)
        dv_acc[keys, :] += dot(p, doms[jj], NN)
        dk_acc[keys, :] += dot(ds, qm[jj], NN)
        dqt[jj] += dot(ks, ds, TN)

    def grad_copy(d):
        return pltpu.make_async_remote_copy(
            src_ref=gsend.at[d - 1], dst_ref=grecv.at[d - 1],
            send_sem=g_send.at[d - 1], recv_sem=g_recv.at[d - 1],
            device_id=((sibling, along(-2), along(-1))[d - 1], g), device_id_type=MESH,
        )

    odd_f = odd.astype(F32)

    for d in (3, 1, 2, 0):
        lo = own - d * ROWS
        if d == SPAN:
            for jj in range(PAIRS):
                unit(jj, jj * PAIR, ROWS - jj * PAIR, 0)
        elif d == 0:
            for jj in range(PAIRS):
                unit(jj, lo, (jj + 1) * PAIR, lo - jj * PAIR)
        else:
            def step(jj, carry):
                unit(jj, lo, ROWS, pl.multiple_of(lo - jj * PAIR, PAIR))
                return carry

            lax.fori_loop(0, PAIRS, step, 0)
        dk = dk_acc[lo : lo + ROWS, :] * SCALE
        dv = dv_acc[lo : lo + ROWS, :]
        if d == 2:
            for e in (1, 3):
                arrived(grecv.at[e - 1], g_recv.at[e - 1])
            dk = dk + grecv[2, 0].astype(F32) + odd_f * grecv[0, 0].astype(F32)
            dv = dv + grecv[2, 1].astype(F32) + odd_f * grecv[0, 1].astype(F32)
        if d > 0:
            gsend[d - 1, 0] = dk.astype(BF16)
            gsend[d - 1, 1] = dv.astype(BF16)
            grad_copy(d).start()

    def finish(jj, carry):
        rows = pl.ds(pl.multiple_of(jj * PAIR, PAIR), PAIR)
        dq = (dqt[jj] * (rls[jj] * SCALE)).T
        dq_ref[rows] = dq.reshape(PAIR, QPK, DIM).astype(BF16)
        return carry

    lax.fori_loop(0, PAIRS, finish, 0)

    dk = dk + (1.0 - odd_f) * grecv[0, 0].astype(F32)
    dv = dv + (1.0 - odd_f) * grecv[0, 1].astype(F32)
    arrived(grecv.at[1], g_recv.at[1])
    dk_ref[...] = (dk + grecv[1, 0].astype(F32)).astype(BF16)
    dv_ref[...] = (dv + grecv[1, 1].astype(F32)).astype(BF16)

    for slot, peer in enumerate(peers):
        for i in range(2):
            kv_copy(i, peer, slot).wait_send()
        wide_copy(2, q_ref, qbuf, peer, slot).wait_send()
        wide_copy(3, do_ref, dobuf, peer, slot).wait_send()
    for i in range(2):
        to_two(i).wait_send()
        to_sibling(i, 0).wait_send()
        to_three(i).wait_send()
    for d in range(1, SPAN + 1):
        grad_copy(d).wait_send()


def put_out(*refs):
    sems = refs[-1]
    n = (len(refs) - 1) // 2
    copies = [pltpu.make_async_copy(refs[i], refs[n + i], sems.at[i]) for i in range(n)]
    for copy in copies:
        copy.start()
    for copy in copies:
        copy.wait()


def local(n_ctx, queries, keys, values, grad_out, segment_ids):
    vmem = pl.BlockSpec(memory_space=pltpu.VMEM)
    anywhere = pl.BlockSpec(memory_space=pl.ANY)
    shapes = ((ROWS, QPK, DIM), (ROWS, QPK, DIM), (ROWS, DIM), (ROWS, DIM))
    results = pl.pallas_call(
        functools.partial(kernel, n_ctx),
        out_shape=tuple(pltpu.VMEM(shape, BF16) for shape in shapes),
        in_specs=[anywhere, anywhere, vmem, vmem, vmem],
        out_specs=(vmem,) * 4,
        scratch_shapes=[
            pltpu.VMEM((PIECE * GROUPS, DIM), F32),
            pltpu.VMEM((GROUPS, 2, PIECE, DIM), BF16),
            pltpu.VMEM((2, WINDOW, DIM), BF16),
            pltpu.VMEM((WINDOW, DIM), BF16),
            pltpu.VMEM((ROWS, DIM), F32),
            pltpu.VMEM((ROWS, QPK, DIM), BF16),
            pltpu.VMEM((ROWS, QPK, DIM), BF16),
            pltpu.VMEM((PAIRS, COLS, DIM), BF16),
            pltpu.VMEM((PAIRS, COLS, DIM), BF16),
            pltpu.VMEM((PAIRS, COLS, DIM), BF16),
            pltpu.VMEM((BAND, COLS), F32),
            pltpu.VMEM((PAIRS, BAND, COLS), BF16),
            pltpu.VMEM((PAIRS, 1, COLS), F32),
            pltpu.VMEM((PAIRS, 1, COLS), F32),
            pltpu.VMEM((PAIRS, DIM, COLS), F32),
            pltpu.VMEM((WINDOW, DIM), F32),
            pltpu.VMEM((WINDOW, DIM), F32),
            pltpu.VMEM((SPAN, 2, ROWS, DIM), BF16),
            pltpu.VMEM((SPAN, 2, ROWS, DIM), BF16),
            pltpu.SemaphoreType.DMA((4, GROUPS - 1)),
            pltpu.SemaphoreType.DMA((4, GROUPS)),
            pltpu.SemaphoreType.DMA((2, SPAN)),
            pltpu.SemaphoreType.DMA((2, SPAN)),
            pltpu.SemaphoreType.DMA((SPAN,)),
            pltpu.SemaphoreType.DMA((SPAN,)),
        ],
        compiler_params=pltpu.CompilerParams(
            collective_id=0, has_side_effects=True, vmem_limit_bytes=56 << 20
        ),
        cost_estimate=pl.CostEstimate(
            flops=12 * DIM * PAIRS * BAND * COLS,
            bytes_accessed=4 * 2 * ROWS * QPK * DIM,
            transcendentals=PAIRS * BAND * COLS,
        ),
    )(
        queries.reshape(PIECE, GROUPS, QPK, DIM),
        grad_out.reshape(PIECE, GROUPS, QPK, DIM),
        keys,
        values,
        segment_ids.reshape(-1, DIM),
    )
    attention, grad_queries, grad_keys, grad_values = pl.pallas_call(
        put_out,
        out_shape=tuple(jax.ShapeDtypeStruct(shape, BF16) for shape in shapes),
        in_specs=[vmem] * 4,
        out_specs=(anywhere,) * 4,
        scratch_shapes=[pltpu.SemaphoreType.DMA((4,))],
    )(*results)
    return (
        attention,
        grad_queries,
        grad_keys.reshape(ROWS, 1, DIM),
        grad_values.reshape(ROWS, 1, DIM),
    )


def solution(mesh):
    rows = P(("ctx", "kvh"), None, None)
    heads = P("ctx", "kvh", None)
    return jax.shard_map(
        functools.partial(local, mesh.shape["ctx"]),
        mesh=mesh,
        in_specs=(rows, rows, rows, rows, P()),
        out_specs=(heads, heads, heads, heads),
        check_vma=False,
    )
```

```python
import functools
import math

import jax
import jax.numpy as jnp
from jax import lax
from jax.experimental import pallas as pl
from jax.experimental.pallas import tpu as pltpu
from jax.sharding import PartitionSpec as P

MESH = pl.DeviceIdType.MESH
SPAN = 3
BIG = 1e30
F32 = jnp.float32
BF16 = jnp.bfloat16

ROWS = 384
PIECE = 48
GROUPS = 8
QPK = 8
DIM = 128
PAIR = 2 * PIECE
PAIRS = ROWS // PAIR
COLS = PAIR * QPK
WINDOW = (SPAN + 1) * ROWS
BAND = SPAN * ROWS + PAIR
SCALE = 1.0 / math.sqrt(DIM)
LOG2E = math.log2(math.e)

NT = (((1,), (1,)), ((), ()))
TN = (((0,), (0,)), ((), ()))
NN = (((1,), (0,)), ((), ()))


def dot(a, b, dims):
    return lax.dot_general(a, b, dims, preferred_element_type=F32)


def kernel(
    n_ctx,
    q_ref, do_ref, k_ref, v_ref, seg_ref,
    att_ref, dq_ref, dk_ref, dv_ref,
    stage, kvsend, kvwin, ohk, ohq, qbuf, dobuf, qm, dom, doms, s_ref, p_all, delta, rls,
    rowl, oall, dqt, dk_acc, dv_acc, gsend, grecv,
    a2a_send, a2a_recv, fwd_send, fwd_recv, g_send, g_recv,
):
    c = lax.axis_index("ctx")
    g = lax.axis_index("kvh")
    x = g // 2
    odd = lax.rem(c, 2)
    sibling = c + 1 - 2 * odd

    def along(steps):
        return lax.rem(c + (steps + n_ctx), n_ctx)

    barrier = pltpu.get_barrier_semaphore()
    for s in range(1, GROUPS):
        pl.semaphore_signal(
            barrier, inc=1, device_id=(c, lax.rem(g + s, GROUPS)), device_id_type=MESH
        )
    for steps in (1, -1, 2, -2):
        pl.semaphore_signal(barrier, inc=1, device_id=(along(steps), g), device_id_type=MESH)

    for i, ref in enumerate((k_ref, v_ref)):
        stage[...] = ref[...].astype(F32).reshape(PIECE * GROUPS, DIM)
        for h in range(GROUPS):
            kvsend[h, i] = stage[pl.ds(h, PIECE, stride=GROUPS), :].astype(BF16)

    pl.semaphore_wait(barrier, GROUPS - 1 + 4)

    own = SPAN * ROWS
    my_rows = pl.ds(pl.multiple_of(g * PIECE, PIECE), PIECE)

    def kv_slot(i):
        return kvwin.at[i, pl.ds(pl.multiple_of(own + g * PIECE, PIECE), PIECE)]

    def kv_copy(i, peer, slot):
        return pltpu.make_async_remote_copy(
            src_ref=kvsend.at[peer, i], dst_ref=kv_slot(i),
            send_sem=a2a_send.at[i, slot], recv_sem=a2a_recv.at[i, g],
            device_id=(c, peer), device_id_type=MESH,
        )

    def wide_copy(i, src, dst, peer, slot):
        return pltpu.make_async_remote_copy(
            src_ref=src.at[:, peer], dst_ref=dst.at[my_rows],
            send_sem=a2a_send.at[i, slot], recv_sem=a2a_recv.at[i, g],
            device_id=(c, peer), device_id_type=MESH,
        )

    peers = []
    z = lax.rem(g, 2)
    for step in (0, 1, 3, 2):
        px = lax.rem(x + step, PAIRS)
        for other in (0, 1):
            if step == 0 and other == 0:
                continue
            peers.append(2 * px + lax.rem(z + other, 2))

    for i in range(2):
        for slot, peer in enumerate(peers):
            kv_copy(i, peer, slot).start()
        pltpu.make_async_copy(kvsend.at[g, i], kv_slot(i), a2a_recv.at[i, g]).start()
    pltpu.make_async_copy(q_ref.at[:, g], qbuf.at[my_rows], a2a_recv.at[2, g]).start()
    pltpu.make_async_copy(do_ref.at[:, g], dobuf.at[my_rows], a2a_recv.at[3, g]).start()
    near = (0, 1, 3)
    far = (2, 4, 5, 6)
    for slot in near:
        wide_copy(2, q_ref, qbuf, peers[slot], slot).start()

    def arrived(ref, sem):
        pltpu.make_async_copy(ref, ref, sem).wait()

    def block(i, d):
        return kvwin.at[i, pl.ds(own - d * ROWS, ROWS)]

    def fwd_copy(i, n, src, d, there):
        return pltpu.make_async_remote_copy(
            src_ref=src, dst_ref=block(i, d),
            send_sem=fwd_send.at[i, n], recv_sem=fwd_recv.at[i, d - 1],
            device_id=(there, g), device_id_type=MESH,
        )

    def to_two(i):
        return fwd_copy(i, 0, block(i, 0), 2, along(2))

    def to_sibling(i, d):
        return fwd_copy(i, 1, block(i, d), 1, sibling)

    def to_three(i):
        return fwd_copy(i, 2, block(i, 2), 3, along(1))

    for i in range(2):
        for j in range(GROUPS):
            arrived(kvwin.at[i, pl.ds(own + j * PIECE, PIECE)], a2a_recv.at[i, j])
        to_two(i).start()

        @pl.when(odd == 0)
        def _():
            to_sibling(i, 0).start()

    for slot in far:
        wide_copy(2, q_ref, qbuf, peers[slot], slot).start()

    tiles = WINDOW // DIM
    seg_rows = n_ctx * ROWS // DIM
    first = c * (ROWS // DIM) + seg_rows - SPAN * (ROWS // DIM)
    number = lax.broadcasted_iota(jnp.int32, (DIM, DIM), 0)
    for i in range(tiles):
        row = seg_ref[pl.ds(lax.rem(first + i, seg_rows), 1), :]
        hot = jnp.where(number == row, 1.0, 0.0).T
        ohk[i * DIM : (i + 1) * DIM, :] = hot.astype(BF16)
        if i >= tiles - ROWS // DIM:
            at = (i - (tiles - ROWS // DIM)) * DIM
            ohq[at : at + DIM, :] = (hot - 1.0) * BIG
    dk_acc[...] = jnp.zeros_like(dk_acc)
    dv_acc[...] = jnp.zeros_like(dv_acc)

    for i in range(2):
        arrived(block(i, 2), fwd_recv.at[i, 1])
        to_three(i).start()

        @pl.when(odd == 1)
        def _():
            to_sibling(i, 2).start()

    for slot, peer in enumerate(peers):
        wide_copy(3, do_ref, dobuf, peer, slot).start()

    for d in (1, 3):
        arrived(block(0, d), fwd_recv.at[0, d - 1])

    def pair(t):
        step = jnp.where(t == 0, 0, jnp.where(t == 1, 3, jnp.where(t == 2, 1, 2)))
        jj = lax.rem(x + step, PAIRS)
        return jj, pl.multiple_of(jj * PAIR, PAIR)

    def pair_arrived(i, buf, jj, base):
        for half in range(2):
            piece = pl.ds(pl.multiple_of(base + half * PIECE, PIECE), PIECE)
            arrived(buf.at[piece], a2a_recv.at[i, 2 * jj + half])

    def forward(t, carry):
        jj, base = pair(t)
        rows = pl.ds(base, PAIR)
        pair_arrived(2, qbuf, jj, base)
        qf = qbuf[rows].astype(F32).reshape(COLS, DIM)
        qb = qf.astype(BF16)
        penalty = jnp.broadcast_to(ohq[rows, :][:, None, :], (PAIR, QPK, DIM))
        qa = jnp.concatenate([qb, penalty.reshape(COLS, DIM).astype(BF16)], axis=1)
        part = BAND // 3
        m8 = None
        for ch in range(3):
            keys = pl.ds(pl.multiple_of(base + ch * part, 32), part)
            ka = jnp.concatenate([kvwin[0, keys, :], ohk[keys, :]], axis=1)
            s = dot(ka, qa, NT)
            if ch == 2:
                tail = s[part - PAIR :]
                key_at = lax.broadcasted_iota(jnp.int32, (PAIR, COLS), 0) * QPK
                col_at = lax.broadcasted_iota(jnp.int32, (PAIR, COLS), 1)
                tail = jnp.where(key_at <= col_at, tail, -BIG)
                s = jnp.concatenate([s[: part - PAIR], tail], axis=0)
            s_ref[ch * part : (ch + 1) * part, :] = s
            top = jnp.max(s.reshape(part // 8, 8, COLS), axis=0)
            m8 = top if m8 is None else jnp.maximum(m8, top)
        m = jnp.max(m8, axis=0, keepdims=True)
        l8 = jnp.zeros((8, COLS), F32)
        for ch in range(BAND // PAIR):
            at = slice(ch * PAIR, (ch + 1) * PAIR)
            e = jnp.exp2((s_ref[at, :] - m) * (SCALE * LOG2E))
            l8 = l8 + jnp.sum(e.reshape(PAIR // 8, 8, COLS), axis=0)
            p_all[jj, at, :] = e.astype(BF16)
        rl = 1.0 / jnp.sum(l8, axis=0, keepdims=True)
        rls[jj] = rl
        by_row = jnp.broadcast_to(rl, (DIM, COLS)).T
        rowl[jj] = by_row
        qm[jj] = (qf * by_row).astype(BF16)

        @pl.when(t == 0)
        def _():
            for d in (1, 3):
                arrived(block(1, d), fwd_recv.at[1, d - 1])

        band = pl.ds(base, BAND)
        ot = dot(kvwin[1, band, :], p_all[jj], TN) * rl
        ot = ot.astype(BF16).astype(F32)
        oall[jj] = ot
        att_ref[rows] = ot.T.reshape(PAIR, QPK, DIM).astype(BF16)
        return carry

    lax.fori_loop(0, PAIRS, forward, 0)

    def take_grad(jj, base):
        pair_arrived(3, dobuf, jj, base)
        dof = dobuf[pl.ds(base, PAIR)].astype(F32).reshape(COLS, DIM)
        dom[...] = dof.astype(BF16)
        doms[...] = (dof * rowl[jj]).astype(BF16)
        delta[...] = jnp.sum(dof.T * oall[jj], axis=0, keepdims=True)
        dqt[...] = jnp.zeros_like(dqt)

    def unit(jj, keys, size, off):
        ks = kvwin[0, keys, :]
        p = p_all[jj, pl.ds(off, size), :]
        dpt = dot(kvwin[1, keys, :], dom[...], NT)
        ds = p * (dpt - delta[...]).astype(BF16)
        dv_acc[keys, :] += dot(p, doms[...], NN)
        dk_acc[keys, :] += dot(ds, qm[jj], NN)
        dqt[...] += dot(ks, ds, TN)

    def put_dq(jj, base):
        dq = (dqt[...] * (rls[jj] * SCALE)).T
        dq_ref[pl.ds(base, PAIR)] = dq.reshape(PAIR, QPK, DIM).astype(BF16)

    def backward(t, carry):
        jj, base = pair(t)
        take_grad(jj, base)
        part = BAND // 3
        for ch in range(3):
            unit(jj, pl.ds(pl.multiple_of(base + ch * part, 32), part), part, ch * part)
        put_dq(jj, base)
        return carry

    lax.fori_loop(0, PAIRS - 1, backward, 0)

    def grad_copy(d):
        return pltpu.make_async_remote_copy(
            src_ref=gsend.at[d - 1], dst_ref=grecv.at[d - 1],
            send_sem=g_send.at[d - 1], recv_sem=g_recv.at[d - 1],
            device_id=((sibling, along(-2), along(-1))[d - 1], g), device_id_type=MESH,
        )

    odd_f = odd.astype(F32)

    jj, base = pair(PAIRS - 1)
    take_grad(jj, base)
    for d in (3, 1, 2, 0):
        lo = own - d * ROWS
        if d in (0, SPAN):
            for v in range(PAIRS):
                lo_key = v * PAIR if d else lo
                size = ROWS - v * PAIR if d else (v + 1) * PAIR
                off = 0 if d else lo - v * PAIR

                @pl.when(jj == v)
                def _():
                    unit(v, pl.ds(lo_key, size), size, off)
        else:
            unit(jj, pl.ds(lo, ROWS), ROWS, pl.multiple_of(lo - jj * PAIR, PAIR))
        dk = dk_acc[lo : lo + ROWS, :] * SCALE
        dv = dv_acc[lo : lo + ROWS, :]
        if d == 2:
            for e in (1, 3):
                arrived(grecv.at[e - 1], g_recv.at[e - 1])
            dk = dk + grecv[2, 0].astype(F32) + odd_f * grecv[0, 0].astype(F32)
            dv = dv + grecv[2, 1].astype(F32) + odd_f * grecv[0, 1].astype(F32)
        if d > 0:
            gsend[d - 1, 0] = dk.astype(BF16)
            gsend[d - 1, 1] = dv.astype(BF16)
            grad_copy(d).start()

    put_dq(jj, base)

    dk = dk + (1.0 - odd_f) * grecv[0, 0].astype(F32)
    dv = dv + (1.0 - odd_f) * grecv[0, 1].astype(F32)
    arrived(grecv.at[1], g_recv.at[1])
    dk_ref[...] = (dk + grecv[1, 0].astype(F32)).astype(BF16)
    dv_ref[...] = (dv + grecv[1, 1].astype(F32)).astype(BF16)

    for slot, peer in enumerate(peers):
        for i in range(2):
            kv_copy(i, peer, slot).wait_send()
        wide_copy(2, q_ref, qbuf, peer, slot).wait_send()
        wide_copy(3, do_ref, dobuf, peer, slot).wait_send()
    for i in range(2):
        to_two(i).wait_send()
        to_sibling(i, 0).wait_send()
        to_three(i).wait_send()
    for d in range(1, SPAN + 1):
        grad_copy(d).wait_send()


def put_out(*refs):
    sems = refs[-1]
    n = (len(refs) - 1) // 2
    copies = [pltpu.make_async_copy(refs[i], refs[n + i], sems.at[i]) for i in range(n)]
    for copy in copies:
        copy.start()
    for copy in copies:
        copy.wait()


def local(n_ctx, queries, keys, values, grad_out, segment_ids):
    vmem = pl.BlockSpec(memory_space=pltpu.VMEM)
    anywhere = pl.BlockSpec(memory_space=pl.ANY)
    shapes = ((ROWS, QPK, DIM), (ROWS, QPK, DIM), (ROWS, DIM), (ROWS, DIM))
    results = pl.pallas_call(
        functools.partial(kernel, n_ctx),
        out_shape=tuple(pltpu.VMEM(shape, BF16) for shape in shapes),
        in_specs=[anywhere, anywhere, vmem, vmem, vmem],
        out_specs=(vmem,) * 4,
        scratch_shapes=[
            pltpu.VMEM((PIECE * GROUPS, DIM), F32),
            pltpu.VMEM((GROUPS, 2, PIECE, DIM), BF16),
            pltpu.VMEM((2, WINDOW, DIM), BF16),
            pltpu.VMEM((WINDOW, DIM), BF16),
            pltpu.VMEM((ROWS, DIM), F32),
            pltpu.VMEM((ROWS, QPK, DIM), BF16),
            pltpu.VMEM((ROWS, QPK, DIM), BF16),
            pltpu.VMEM((PAIRS, COLS, DIM), BF16),
            pltpu.VMEM((COLS, DIM), BF16),
            pltpu.VMEM((COLS, DIM), BF16),
            pltpu.VMEM((BAND, COLS), F32),
            pltpu.VMEM((PAIRS, BAND, COLS), BF16),
            pltpu.VMEM((1, COLS), F32),
            pltpu.VMEM((PAIRS, 1, COLS), F32),
            pltpu.VMEM((PAIRS, COLS, DIM), F32),
            pltpu.VMEM((PAIRS, DIM, COLS), F32),
            pltpu.VMEM((DIM, COLS), F32),
            pltpu.VMEM((WINDOW, DIM), F32),
            pltpu.VMEM((WINDOW, DIM), F32),
            pltpu.VMEM((SPAN, 2, ROWS, DIM), BF16),
            pltpu.VMEM((SPAN, 2, ROWS, DIM), BF16),
            pltpu.SemaphoreType.DMA((4, GROUPS - 1)),
            pltpu.SemaphoreType.DMA((4, GROUPS)),
            pltpu.SemaphoreType.DMA((2, SPAN)),
            pltpu.SemaphoreType.DMA((2, SPAN)),
            pltpu.SemaphoreType.DMA((SPAN,)),
            pltpu.SemaphoreType.DMA((SPAN,)),
        ],
        compiler_params=pltpu.CompilerParams(
            collective_id=0, has_side_effects=True, vmem_limit_bytes=56 << 20
        ),
        cost_estimate=pl.CostEstimate(
            flops=12 * DIM * PAIRS * BAND * COLS,
            bytes_accessed=4 * 2 * ROWS * QPK * DIM,
            transcendentals=PAIRS * BAND * COLS,
        ),
    )(
        queries.reshape(PIECE, GROUPS, QPK, DIM),
        grad_out.reshape(PIECE, GROUPS, QPK, DIM),
        keys,
        values,
        segment_ids.reshape(-1, DIM),
    )
    attention, grad_queries, grad_keys, grad_values = pl.pallas_call(
        put_out,
        out_shape=tuple(jax.ShapeDtypeStruct(shape, BF16) for shape in shapes),
        in_specs=[anywhere] * 4,
        out_specs=(anywhere,) * 4,
        scratch_shapes=[pltpu.SemaphoreType.DMA((4,))],
        compiler_params=pltpu.CompilerParams(vmem_limit_bytes=1 << 20),
    )(*[pltpu.with_memory_space_constraint(r, pltpu.VMEM) for r in results])
    return (
        attention,
        grad_queries,
        grad_keys.reshape(ROWS, 1, DIM),
        grad_values.reshape(ROWS, 1, DIM),
    )


def solution(mesh):
    rows = P(("ctx", "kvh"), None, None)
    heads = P("ctx", "kvh", None)
    return jax.shard_map(
        functools.partial(local, mesh.shape["ctx"]),
        mesh=mesh,
        in_specs=(rows, rows, rows, rows, P()),
        out_specs=(heads, heads, heads, heads),
        check_vma=False,
    )
```

```python
import functools
import math

import jax
import jax.numpy as jnp
from jax import lax
from jax.experimental import pallas as pl
from jax.experimental.pallas import tpu as pltpu
from jax.sharding import PartitionSpec as P

MESH = pl.DeviceIdType.MESH
SPAN = 3
GROUP = 16
BIG = 1e30
F32 = jnp.float32
BF16 = jnp.bfloat16

ROWS = 384
PIECE = 48
GROUPS = 8
QPK = 8
DIM = 128
PAIR = 2 * PIECE
PAIRS = ROWS // PAIR
COLS = PAIR * QPK
WINDOW = (SPAN + 1) * ROWS
BAND = SPAN * ROWS + PAIR
SCALE = 1.0 / math.sqrt(DIM)
LOG2E = math.log2(math.e)

NT = (((1,), (1,)), ((), ()))
TN = (((0,), (0,)), ((), ()))
NN = (((1,), (0,)), ((), ()))


def dot(a, b, dims):
    return lax.dot_general(a, b, dims, preferred_element_type=F32)


def kernel(
    n_ctx,
    q_ref, do_ref, k_ref, v_ref, seg_ref,
    att_ref, dq_ref, dk_ref, dv_ref,
    stage, kvsend, kvwin, ohk, ohq, qbuf, dobuf, qm, dom, doms, s_ref, p_all, delta, rls,
    rowl, oall, dqt, dk_acc, dv_acc, gsend, grecv, rbuf,
    a2a_send, a2a_recv, rel_send, rel_recv, fwd_send, fwd_recv, g_send, g_recv,
):
    c = lax.axis_index("ctx")
    g = lax.axis_index("kvh")
    x = g // 2
    odd = lax.rem(c, 2)
    sibling = c + 1 - 2 * odd

    barrier = pltpu.get_barrier_semaphore()
    for s in range(1, GROUPS):
        pl.semaphore_signal(
            barrier, inc=1, device_id=(c, lax.rem(g + s, GROUPS)), device_id_type=MESH
        )

    def before(d):
        return c >= d

    def behind(d):
        return c + d < n_ctx

    for d in (1, 2):
        for there, exists in ((c + d, behind(d)), (c - d, before(d))):
            @pl.when(exists)
            def _():
                pl.semaphore_signal(barrier, inc=1, device_id=(there, g), device_id_type=MESH)

    place = lax.rem(c, GROUP)
    first_y, last_y = place < 2, place >= GROUP - 2
    over_on = last_y & behind(2)
    relay_on = last_y & before(GROUP)
    greet = (
        (c + GROUP, over_on),
        (c - GROUP, relay_on),
        (c + GROUP - 2, first_y & before(GROUP)),
        (c - GROUP + 2, relay_on),
        (c + GROUP - 1, first_y & (odd == 0) & before(GROUP)),
        (c - GROUP + 1, relay_on & (odd == 1)),
    )
    greet = greet if n_ctx > GROUP else ()
    for there, exists in greet:
        @pl.when(exists)
        def _():
            pl.semaphore_signal(barrier, inc=1, device_id=(there, g), device_id_type=MESH)

    for i, ref in enumerate((k_ref, v_ref)):
        stage[...] = ref[...].astype(F32).reshape(PIECE * GROUPS, DIM)
        for h in range(GROUPS):
            kvsend[h, i] = stage[pl.ds(h, PIECE, stride=GROUPS), :].astype(BF16)

    partners = sum(e(d).astype(jnp.int32) for e in (before, behind) for d in (1, 2))
    partners = partners + sum(exists.astype(jnp.int32) for _, exists in greet)
    pl.semaphore_wait(barrier, partners + (GROUPS - 1))

    own = SPAN * ROWS
    my_rows = pl.ds(pl.multiple_of(g * PIECE, PIECE), PIECE)

    def kv_slot(i):
        return kvwin.at[i, pl.ds(pl.multiple_of(own + g * PIECE, PIECE), PIECE)]

    def kv_copy(i, peer, slot):
        return pltpu.make_async_remote_copy(
            src_ref=kvsend.at[peer, i], dst_ref=kv_slot(i),
            send_sem=a2a_send.at[i, slot], recv_sem=a2a_recv.at[i, g],
            device_id=(c, peer), device_id_type=MESH,
        )

    def wide_copy(i, src, dst, peer, slot):
        return pltpu.make_async_remote_copy(
            src_ref=src.at[:, peer], dst_ref=dst.at[my_rows],
            send_sem=a2a_send.at[i, slot], recv_sem=a2a_recv.at[i, g],
            device_id=(c, peer), device_id_type=MESH,
        )

    peers = []
    z = lax.rem(g, 2)
    for step in (0, 1, 3, 2):
        px = lax.rem(x + step, PAIRS)
        for other in (0, 1):
            if step == 0 and other == 0:
                continue
            peers.append(2 * px + lax.rem(z + other, 2))

    wide = ((q_ref, qbuf), (do_ref, dobuf))

    def send_wide(i, slots):
        for slot in slots:
            wide_copy(i, *wide[i - 2], peers[slot], slot).start()

    def arrived(ref, sem):
        pltpu.make_async_copy(ref, ref, sem).wait()

    for i in range(2):
        for slot, peer in enumerate(peers):
            kv_copy(i, peer, slot).start()
        pltpu.make_async_copy(kvsend.at[g, i], kv_slot(i), a2a_recv.at[i, g]).start()
    send_wide(2, (0, 1, 3))
    pltpu.make_async_copy(q_ref.at[:, g], qbuf.at[my_rows], a2a_recv.at[2, g]).start()
    pltpu.make_async_copy(do_ref.at[:, g], dobuf.at[my_rows], a2a_recv.at[3, g]).start()

    def block(i, d):
        return kvwin.at[i, pl.ds(own - d * ROWS, ROWS)]

    def fwd_copy(i, n, src, d, there):
        return pltpu.make_async_remote_copy(
            src_ref=src, dst_ref=block(i, d),
            send_sem=fwd_send.at[i, n], recv_sem=fwd_recv.at[i, d - 1],
            device_id=(there, g), device_id_type=MESH,
        )

    def to_two(i):
        return fwd_copy(i, 0, block(i, 0), 2, c + 2)

    def to_sibling(i, d):
        return fwd_copy(i, 1, block(i, d), 1, sibling)

    def to_three(i):
        return fwd_copy(i, 2, block(i, 2), 3, c + 1)

    def to_relay(n):
        return pltpu.make_async_remote_copy(
            src_ref=block(0, 2 * n), dst_ref=rbuf.at[n],
            send_sem=fwd_send.at[0, 2 * n], recv_sem=rel_recv.at[n],
            device_id=(c + GROUP, g), device_id_type=MESH,
        )

    def from_relay(n):
        return pltpu.make_async_remote_copy(
            src_ref=rbuf.at[n], dst_ref=block(0, 2 + n),
            send_sem=rel_send.at[n], recv_sem=fwd_recv.at[0, 1 + n],
            device_id=(c - GROUP + 2 - n, g), device_id_type=MESH,
        )

    def start_on(i, n, plain, valid):
        if i == 0 and greet:
            @pl.when(valid & over_on)
            def _():
                to_relay(n).start()

            valid = valid & jnp.logical_not(over_on)

        @pl.when(valid)
        def _():
            plain(i).start()

    two = behind(2)
    three = before(2) & behind(1)
    even_sibling = odd == 0
    odd_sibling = (odd == 1) & before(2)

    for i in range(2):
        for j in range(GROUPS):
            arrived(kvwin.at[i, pl.ds(own + j * PIECE, PIECE)], a2a_recv.at[i, j])

        start_on(i, 0, to_two, two)

        @pl.when(even_sibling)
        def _():
            to_sibling(i, 0).start()

    send_wide(2, (2, 4, 5, 6))

    tiles = WINDOW // DIM
    seg_rows = n_ctx * ROWS // DIM
    first = c * (ROWS // DIM) + seg_rows - SPAN * (ROWS // DIM)
    number = lax.broadcasted_iota(jnp.int32, (DIM, DIM), 0)
    for i in range(tiles):
        row = seg_ref[pl.ds(lax.rem(first + i, seg_rows), 1), :]
        hot = jnp.where(number == row, 1.0, 0.0).T
        ohk[i * DIM : (i + 1) * DIM, :] = hot.astype(BF16)
        if i >= tiles - ROWS // DIM:
            at = (i - (tiles - ROWS // DIM)) * DIM
            ohq[at : at + DIM, :] = (hot - 1.0) * BIG
    dk_acc[...] = jnp.zeros_like(dk_acc)
    dv_acc[...] = jnp.zeros_like(dv_acc)

    for d in (1, 2, 3):
        @pl.when(jnp.logical_not(before(d)))
        def _():
            kvwin[:, own - d * ROWS : own - (d - 1) * ROWS, :] = jnp.zeros((2, ROWS, DIM), BF16)

    def block_arrived(i, d):
        @pl.when(before(d))
        def _():
            arrived(block(i, d), fwd_recv.at[i, d - 1])

    for i in range(2):
        block_arrived(i, 2)

        if i == 0 and greet:
            start_on(0, 1, to_three, three & (odd == 1))

            @pl.when(three & (odd == 0))
            def _():
                to_three(0).start()
        else:
            start_on(i, 1, to_three, three)

        @pl.when(odd_sibling)
        def _():
            to_sibling(i, 2).start()

    if greet:
        for n, where in ((0, relay_on), (1, relay_on & (odd == 1))):
            @pl.when(where)
            def _():
                arrived(rbuf.at[n], rel_recv.at[n])
                from_relay(n).start()

    send_wide(3, range(GROUPS - 1))

    for d in (1, 3):
        block_arrived(0, d)

    def pair(t):
        step = jnp.where(t == 0, 0, jnp.where(t == 1, 3, jnp.where(t == 2, 1, 2)))
        jj = lax.rem(x + step, PAIRS)
        return jj, pl.multiple_of(jj * PAIR, PAIR)

    def pair_arrived(i, buf, jj, base):
        for half in range(2):
            piece = pl.ds(pl.multiple_of(base + half * PIECE, PIECE), PIECE)
            arrived(buf.at[piece], a2a_recv.at[i, 2 * jj + half])

    def forward(t, carry):
        jj, base = pair(t)
        rows = pl.ds(base, PAIR)
        pair_arrived(2, qbuf, jj, base)
        qf = qbuf[rows].astype(F32).reshape(COLS, DIM)
        qb = qf.astype(BF16)
        penalty = jnp.broadcast_to(ohq[rows, :][:, None, :], (PAIR, QPK, DIM))
        qa = jnp.concatenate([qb, penalty.reshape(COLS, DIM).astype(BF16)], axis=1)
        part = BAND // 3
        m8 = None
        for ch in range(3):
            keys = pl.ds(pl.multiple_of(base + ch * part, 32), part)
            ka = jnp.concatenate([kvwin[0, keys, :], ohk[keys, :]], axis=1)
            s = dot(ka, qa, NT)
            if ch == 2:
                tail = s[part - PAIR :]
                key_at = lax.broadcasted_iota(jnp.int32, (PAIR, COLS), 0) * QPK
                col_at = lax.broadcasted_iota(jnp.int32, (PAIR, COLS), 1)
                tail = jnp.where(key_at <= col_at, tail, -BIG)
                s = jnp.concatenate([s[: part - PAIR], tail], axis=0)
            s_ref[ch * part : (ch + 1) * part, :] = s
            top = jnp.max(s.reshape(part // 8, 8, COLS), axis=0)
            m8 = top if m8 is None else jnp.maximum(m8, top)
        m = jnp.max(m8, axis=0, keepdims=True)
        l8 = jnp.zeros((8, COLS), F32)
        for ch in range(BAND // PAIR):
            at = slice(ch * PAIR, (ch + 1) * PAIR)
            e = jnp.exp2((s_ref[at, :] - m) * (SCALE * LOG2E))
            l8 = l8 + jnp.sum(e.reshape(PAIR // 8, 8, COLS), axis=0)
            p_all[jj, at, :] = e.astype(BF16)
        rl = 1.0 / jnp.sum(l8, axis=0, keepdims=True)
        rls[jj] = rl
        by_row = jnp.broadcast_to(rl, (DIM, COLS)).T
        rowl[jj] = by_row
        qm[jj] = (qf * by_row).astype(BF16)

        @pl.when(t == 0)
        def _():
            for d in (1, 3):
                block_arrived(1, d)

        band = pl.ds(base, BAND)
        ot = dot(kvwin[1, band, :], p_all[jj], TN) * rl
        ot = ot.astype(BF16).astype(F32)
        oall[jj] = ot
        att_ref[rows] = ot.T.reshape(PAIR, QPK, DIM).astype(BF16)
        return carry

    lax.fori_loop(0, PAIRS, forward, 0)

    def take_grad(t, carry):
        jj, base = pair(t)
        pair_arrived(3, dobuf, jj, base)
        dof = dobuf[pl.ds(base, PAIR)].astype(F32).reshape(COLS, DIM)
        dom[jj] = dof.astype(BF16)
        doms[jj] = (dof * rowl[jj]).astype(BF16)
        delta[jj] = jnp.sum(dof.T * oall[jj], axis=0, keepdims=True)
        return carry

    lax.fori_loop(0, PAIRS, take_grad, 0)

    def unit(jj, lo, size, off, first=False):
        keys = pl.ds(lo, size)
        ks = kvwin[0, keys, :]
        p = p_all[jj, pl.ds(off, size), :]
        dpt = dot(kvwin[1, keys, :], dom[jj], NT)
        ds = p * (dpt - delta[jj]).astype(BF16)
        dv_acc[keys, :] += dot(p, doms[jj], NN)
        dk_acc[keys, :] += dot(ds, qm[jj], NN)
        if first:
            dqt[jj] = dot(ks, ds, TN)
        else:
            dqt[jj] += dot(ks, ds, TN)

    def put_dq(jj, carry):
        dq = (dqt[jj] * (rls[jj] * SCALE)).T
        rows = pl.ds(pl.multiple_of(jj * PAIR, PAIR), PAIR)
        dq_ref[rows] = dq.reshape(PAIR, QPK, DIM).astype(BF16)
        return carry

    def grad_copy(d):
        return pltpu.make_async_remote_copy(
            src_ref=gsend.at[d - 1], dst_ref=grecv.at[d - 1],
            send_sem=g_send.at[d - 1], recv_sem=g_recv.at[d - 1],
            device_id=((sibling, c - 2, c - 1)[d - 1], g), device_id_type=MESH,
        )

    odd_f = odd.astype(F32)
    sends = ((odd == 1) | before(2), before(2), before(3))
    takes = ((odd == 0) | before(3), behind(2), behind(1) & before(2))

    def grad_arrived(d):
        @pl.when(takes[d - 1])
        def _():
            arrived(grecv.at[d - 1], g_recv.at[d - 1])

        @pl.when(jnp.logical_not(takes[d - 1]))
        def _():
            grecv[d - 1] = jnp.zeros((2, ROWS, DIM), BF16)

    def terms(d):
        rows = slice(own - d * ROWS, own - d * ROWS + ROWS)
        return dk_acc[rows, :] * SCALE, dv_acc[rows, :]

    def send_terms(d, with_sibling=False):
        dk, dv = terms(d)
        if d == 2:
            grad_arrived(3)
            dk = dk + grecv[2, 0].astype(F32)
            dv = dv + grecv[2, 1].astype(F32)
        if with_sibling:
            dk = dk + grecv[0, 0].astype(F32)
            dv = dv + grecv[0, 1].astype(F32)
        gsend[d - 1, 0] = dk.astype(BF16)
        gsend[d - 1, 1] = dv.astype(BF16)

        @pl.when(sends[d - 1])
        def _():
            grad_copy(d).start()

    def whole_block(d):
        lo = pl.multiple_of(own - d * ROWS, ROWS)

        def step(jj, carry):
            unit(jj, lo, ROWS, pl.multiple_of(lo - jj * PAIR, PAIR))
            return carry

        lax.fori_loop(0, PAIRS, step, 0)

    for jj in range(PAIRS):
        unit(jj, jj * PAIR, ROWS - jj * PAIR, 0, first=True)
    send_terms(3)
    whole_block(1 + odd)

    @pl.when(odd == 0)
    def _():
        send_terms(1)

    @pl.when(odd == 1)
    def _():
        grad_arrived(1)
        send_terms(2, with_sibling=True)

    whole_block(2 - odd)

    @pl.when(odd == 0)
    def _():
        send_terms(2)

    @pl.when(odd == 1)
    def _():
        send_terms(1)

    for jj in range(PAIRS):
        unit(jj, own, (jj + 1) * PAIR, own - jj * PAIR)

    lax.fori_loop(0, PAIRS, put_dq, 0)

    dk, dv = terms(0)

    @pl.when(odd == 0)
    def _():
        grad_arrived(1)

    dk = dk + (1.0 - odd_f) * grecv[0, 0].astype(F32)
    dv = dv + (1.0 - odd_f) * grecv[0, 1].astype(F32)
    grad_arrived(2)
    dk_ref[...] = (dk + grecv[1, 0].astype(F32)).astype(BF16)
    dv_ref[...] = (dv + grecv[1, 1].astype(F32)).astype(BF16)

    for slot, peer in enumerate(peers):
        for i in range(2):
            kv_copy(i, peer, slot).wait_send()
            wide_copy(2 + i, *wide[i], peer, slot).wait_send()
    for i in range(2):
        for copy, sent in (
            (to_two(i), two), (to_sibling(i, 0), even_sibling | odd_sibling), (to_three(i), three)
        ):
            @pl.when(sent)
            def _():
                copy.wait_send()
    for d in range(1, SPAN + 1):
        @pl.when(sends[d - 1])
        def _():
            grad_copy(d).wait_send()
    if greet:
        for n, where in ((0, relay_on), (1, relay_on & (odd == 1))):
            @pl.when(where)
            def _():
                from_relay(n).wait_send()


def put_out(*refs):
    sems = refs[-1]
    n = (len(refs) - 1) // 2
    copies = [pltpu.make_async_copy(refs[i], refs[n + i], sems.at[i]) for i in range(n)]
    for copy in copies:
        copy.start()
    for copy in copies:
        copy.wait()


def local(n_ctx, queries, keys, values, grad_out, segment_ids):
    vmem = pl.BlockSpec(memory_space=pltpu.VMEM)
    anywhere = pl.BlockSpec(memory_space=pl.ANY)
    shapes = ((ROWS, QPK, DIM), (ROWS, QPK, DIM), (ROWS, DIM), (ROWS, DIM))
    results = pl.pallas_call(
        functools.partial(kernel, n_ctx),
        out_shape=tuple(pltpu.VMEM(shape, BF16) for shape in shapes),
        in_specs=[anywhere, anywhere, vmem, vmem, vmem],
        out_specs=(vmem,) * 4,
        scratch_shapes=[
            pltpu.VMEM((PIECE * GROUPS, DIM), F32),
            pltpu.VMEM((GROUPS, 2, PIECE, DIM), BF16),
            pltpu.VMEM((2, WINDOW, DIM), BF16),
            pltpu.VMEM((WINDOW, DIM), BF16),
            pltpu.VMEM((ROWS, DIM), F32),
            pltpu.VMEM((ROWS, QPK, DIM), BF16),
            pltpu.VMEM((ROWS, QPK, DIM), BF16),
            pltpu.VMEM((PAIRS, COLS, DIM), BF16),
            pltpu.VMEM((PAIRS, COLS, DIM), BF16),
            pltpu.VMEM((PAIRS, COLS, DIM), BF16),
            pltpu.VMEM((BAND, COLS), F32),
            pltpu.VMEM((PAIRS, BAND, COLS), BF16),
            pltpu.VMEM((PAIRS, 1, COLS), F32),
            pltpu.VMEM((PAIRS, 1, COLS), F32),
            pltpu.VMEM((PAIRS, COLS, DIM), F32),
            pltpu.VMEM((PAIRS, DIM, COLS), F32),
            pltpu.VMEM((PAIRS, DIM, COLS), F32),
            pltpu.VMEM((WINDOW, DIM), F32),
            pltpu.VMEM((WINDOW, DIM), F32),
            pltpu.VMEM((SPAN, 2, ROWS, DIM), BF16),
            pltpu.VMEM((SPAN, 2, ROWS, DIM), BF16),
            pltpu.VMEM((2, ROWS, DIM), BF16),
            pltpu.SemaphoreType.DMA((4, GROUPS - 1)),
            pltpu.SemaphoreType.DMA((4, GROUPS)),
            pltpu.SemaphoreType.DMA((2,)),
            pltpu.SemaphoreType.DMA((2,)),
            pltpu.SemaphoreType.DMA((2, SPAN)),
            pltpu.SemaphoreType.DMA((2, SPAN)),
            pltpu.SemaphoreType.DMA((SPAN,)),
            pltpu.SemaphoreType.DMA((SPAN,)),
        ],
        compiler_params=pltpu.CompilerParams(
            collective_id=0, has_side_effects=True, vmem_limit_bytes=56 << 20
        ),
        cost_estimate=pl.CostEstimate(
            flops=12 * DIM * PAIRS * BAND * COLS,
            bytes_accessed=4 * 2 * ROWS * QPK * DIM,
            transcendentals=PAIRS * BAND * COLS,
        ),
    )(
        queries.reshape(PIECE, GROUPS, QPK, DIM),
        grad_out.reshape(PIECE, GROUPS, QPK, DIM),
        keys,
        values,
        segment_ids.reshape(-1, DIM),
    )
    attention, grad_queries, grad_keys, grad_values = pl.pallas_call(
        put_out,
        out_shape=tuple(jax.ShapeDtypeStruct(shape, BF16) for shape in shapes),
        in_specs=[anywhere] * 4,
        out_specs=(anywhere,) * 4,
        scratch_shapes=[pltpu.SemaphoreType.DMA((4,))],
        compiler_params=pltpu.CompilerParams(vmem_limit_bytes=1 << 20),
    )(*[pltpu.with_memory_space_constraint(r, pltpu.VMEM) for r in results])
    return (
        attention,
        grad_queries,
        grad_keys.reshape(ROWS, 1, DIM),
        grad_values.reshape(ROWS, 1, DIM),
    )


def solution(mesh):
    rows = P(("ctx", "kvh"), None, None)
    heads = P("ctx", "kvh", None)
    return jax.shard_map(
        functools.partial(local, mesh.shape["ctx"]),
        mesh=mesh,
        in_specs=(rows, rows, rows, rows, P()),
        out_specs=(heads, heads, heads, heads),
        check_vma=False,
    )
```

```python
import functools
import math

import jax
import jax.numpy as jnp
from jax import lax
from jax.experimental import pallas as pl
from jax.experimental.pallas import tpu as pltpu
from jax.sharding import PartitionSpec as P

MESH = pl.DeviceIdType.MESH
SPAN = 3
GROUP = 16
BIG = 1e30
F32 = jnp.float32
BF16 = jnp.bfloat16

ROWS = 384
PIECE = 48
GROUPS = 8
QPK = 8
DIM = 128
PAIR = 2 * PIECE
PAIRS = ROWS // PAIR
COLS = PAIR * QPK
WINDOW = (SPAN + 1) * ROWS
BAND = SPAN * ROWS + PAIR
SCALE = 1.0 / math.sqrt(DIM)
LOG2E = math.log2(math.e)

NT = (((1,), (1,)), ((), ()))
TN = (((0,), (0,)), ((), ()))
NN = (((1,), (0,)), ((), ()))


def dot(a, b, dims):
    return lax.dot_general(a, b, dims, preferred_element_type=F32)


def kernel(
    n_ctx,
    q_ref, do_ref, k_ref, v_ref, seg_ref,
    att_ref, dq_ref, dk_ref, dv_ref,
    stage, kvsend, kvwin, ohk, ohq, qbuf, dobuf, qm, dom, doms, s_ref, p_all, delta, rls,
    rowl, oall, dqt, dk_acc, dv_acc, gsend, grecv, rbuf,
    a2a_send, a2a_recv, rel_send, rel_recv, fwd_send, fwd_recv, g_send, g_recv,
):
    c = lax.axis_index("ctx")
    g = lax.axis_index("kvh")
    x = g // 2
    odd = lax.rem(c, 2)
    sibling = c + 1 - 2 * odd

    barrier = pltpu.get_barrier_semaphore()
    for s in range(1, GROUPS):
        pl.semaphore_signal(
            barrier, inc=1, device_id=(c, lax.rem(g + s, GROUPS)), device_id_type=MESH
        )

    def before(d):
        return c >= d

    def behind(d):
        return c + d < n_ctx

    for d in (1, 2):
        for there, exists in ((c + d, behind(d)), (c - d, before(d))):
            @pl.when(exists)
            def _():
                pl.semaphore_signal(barrier, inc=1, device_id=(there, g), device_id_type=MESH)

    place = lax.rem(c, GROUP)
    first_y, last_y = place < 2, place >= GROUP - 2
    over_on = last_y & behind(2)
    relay_on = last_y & before(GROUP)
    greet = (
        (c + GROUP, over_on),
        (c - GROUP, relay_on),
        (c + GROUP - 2, first_y & before(GROUP)),
        (c - GROUP + 2, relay_on),
        (c + GROUP - 1, first_y & (odd == 0) & before(GROUP)),
        (c - GROUP + 1, relay_on & (odd == 1)),
    )
    greet = greet if n_ctx > GROUP else ()
    for there, exists in greet:
        @pl.when(exists)
        def _():
            pl.semaphore_signal(barrier, inc=1, device_id=(there, g), device_id_type=MESH)

    for i, ref in enumerate((k_ref, v_ref)):
        stage[...] = ref[...].astype(F32).reshape(PIECE * GROUPS, DIM)
        for h in range(GROUPS):
            kvsend[h, i] = stage[pl.ds(h, PIECE, stride=GROUPS), :].astype(BF16)

    partners = sum(e(d).astype(jnp.int32) for e in (before, behind) for d in (1, 2))
    partners = partners + sum(exists.astype(jnp.int32) for _, exists in greet)
    pl.semaphore_wait(barrier, partners + (GROUPS - 1))

    own = SPAN * ROWS
    my_rows = pl.ds(pl.multiple_of(g * PIECE, PIECE), PIECE)

    def kv_slot(i):
        return kvwin.at[i, pl.ds(pl.multiple_of(own + g * PIECE, PIECE), PIECE)]

    def kv_copy(i, peer, slot):
        return pltpu.make_async_remote_copy(
            src_ref=kvsend.at[peer, i], dst_ref=kv_slot(i),
            send_sem=a2a_send.at[i, slot], recv_sem=a2a_recv.at[i, g],
            device_id=(c, peer), device_id_type=MESH,
        )

    def wide_copy(i, src, dst, peer, slot):
        return pltpu.make_async_remote_copy(
            src_ref=src.at[:, peer], dst_ref=dst.at[my_rows],
            send_sem=a2a_send.at[i, slot], recv_sem=a2a_recv.at[i, g],
            device_id=(c, peer), device_id_type=MESH,
        )

    peers = []
    z = lax.rem(g, 2)
    for step in (0, 1, 3, 2):
        px = lax.rem(x + step, PAIRS)
        for other in (0, 1):
            if step == 0 and other == 0:
                continue
            peers.append(2 * px + lax.rem(z + other, 2))

    wide = ((q_ref, qbuf), (do_ref, dobuf))

    def send_wide(i, slots):
        for slot in slots:
            wide_copy(i, *wide[i - 2], peers[slot], slot).start()

    def arrived(ref, sem):
        pltpu.make_async_copy(ref, ref, sem).wait()

    for i in range(2):
        for slot, peer in enumerate(peers):
            kv_copy(i, peer, slot).start()
        pltpu.make_async_copy(kvsend.at[g, i], kv_slot(i), a2a_recv.at[i, g]).start()
    send_wide(2, (0, 1, 3))
    pltpu.make_async_copy(q_ref.at[:, g], qbuf.at[my_rows], a2a_recv.at[2, g]).start()
    pltpu.make_async_copy(do_ref.at[:, g], dobuf.at[my_rows], a2a_recv.at[3, g]).start()

    def block(i, d):
        return kvwin.at[i, pl.ds(own - d * ROWS, ROWS)]

    def fwd_copy(i, n, src, d, there):
        return pltpu.make_async_remote_copy(
            src_ref=src, dst_ref=block(i, d),
            send_sem=fwd_send.at[i, n], recv_sem=fwd_recv.at[i, d - 1],
            device_id=(there, g), device_id_type=MESH,
        )

    def to_two(i):
        return fwd_copy(i, 0, block(i, 0), 2, c + 2)

    def to_sibling(i, d):
        return fwd_copy(i, 1, block(i, d), 1, sibling)

    def to_three(i):
        return fwd_copy(i, 2, block(i, 2), 3, c + 1)

    def to_relay(n):
        return pltpu.make_async_remote_copy(
            src_ref=block(0, 2 * n), dst_ref=rbuf.at[n],
            send_sem=fwd_send.at[0, 2 * n], recv_sem=rel_recv.at[n],
            device_id=(c + GROUP, g), device_id_type=MESH,
        )

    def from_relay(n):
        return pltpu.make_async_remote_copy(
            src_ref=rbuf.at[n], dst_ref=block(0, 2 + n),
            send_sem=rel_send.at[n], recv_sem=fwd_recv.at[0, 1 + n],
            device_id=(c - GROUP + 2 - n, g), device_id_type=MESH,
        )

    def start_on(i, n, plain, valid):
        if i == 0 and greet:
            @pl.when(valid & over_on)
            def _():
                to_relay(n).start()

            valid = valid & jnp.logical_not(over_on)

        @pl.when(valid)
        def _():
            plain(i).start()

    two = behind(2)
    three = before(2) & behind(1)
    even_sibling = odd == 0
    odd_sibling = (odd == 1) & before(2)

    for i in range(2):
        for j in range(GROUPS):
            arrived(kvwin.at[i, pl.ds(own + j * PIECE, PIECE)], a2a_recv.at[i, j])

        start_on(i, 0, to_two, two)

        @pl.when(even_sibling)
        def _():
            to_sibling(i, 0).start()

    send_wide(2, (2, 4, 5, 6))

    tiles = WINDOW // DIM
    seg_rows = n_ctx * ROWS // DIM
    first = c * (ROWS // DIM) + seg_rows - SPAN * (ROWS // DIM)
    number = lax.broadcasted_iota(jnp.int32, (DIM, DIM), 0)
    for i in range(tiles):
        row = seg_ref[pl.ds(lax.rem(first + i, seg_rows), 1), :]
        hot = jnp.where(number == row, 1.0, 0.0).T
        ohk[i * DIM : (i + 1) * DIM, :] = hot.astype(BF16)
        if i >= tiles - ROWS // DIM:
            at = (i - (tiles - ROWS // DIM)) * DIM
            ohq[at : at + DIM, :] = (hot - 1.0) * BIG
    dk_acc[...] = jnp.zeros_like(dk_acc)
    dv_acc[...] = jnp.zeros_like(dv_acc)

    for d in (1, 2, 3):
        @pl.when(jnp.logical_not(before(d)))
        def _():
            kvwin[:, own - d * ROWS : own - (d - 1) * ROWS, :] = jnp.zeros((2, ROWS, DIM), BF16)

    def block_arrived(i, d):
        @pl.when(before(d))
        def _():
            arrived(block(i, d), fwd_recv.at[i, d - 1])

    for i in range(2):
        block_arrived(i, 2)

        if i == 0 and greet:
            start_on(0, 1, to_three, three & (odd == 1))

            @pl.when(three & (odd == 0))
            def _():
                to_three(0).start()
        else:
            start_on(i, 1, to_three, three)

        @pl.when(odd_sibling)
        def _():
            to_sibling(i, 2).start()

    if greet:
        for n, where in ((0, relay_on), (1, relay_on & (odd == 1))):
            @pl.when(where)
            def _():
                arrived(rbuf.at[n], rel_recv.at[n])
                from_relay(n).start()

    send_wide(3, range(GROUPS - 1))

    for d in (1, 3):
        block_arrived(0, d)

    def pair(t):
        step = jnp.where(t == 0, 0, jnp.where(t == 1, 3, jnp.where(t == 2, 1, 2)))
        jj = lax.rem(x + step, PAIRS)
        return jj, pl.multiple_of(jj * PAIR, PAIR)

    def pair_arrived(i, buf, jj, base):
        for half in range(2):
            piece = pl.ds(pl.multiple_of(base + half * PIECE, PIECE), PIECE)
            arrived(buf.at[piece], a2a_recv.at[i, 2 * jj + half])

    part = BAND // 3

    def load_pair(t):
        jj, base = pair(t)
        rows = pl.ds(base, PAIR)
        pair_arrived(2, qbuf, jj, base)
        qf = qbuf[rows].astype(F32).reshape(COLS, DIM)
        penalty = jnp.broadcast_to(ohq[rows, :][:, None, :], (PAIR, QPK, DIM))
        penalty = penalty.reshape(COLS, DIM).astype(BF16)
        return jj, base, qf, jnp.concatenate([qf.astype(BF16), penalty], axis=1)

    def scores(work, buf, ch):
        _, base, _, qa = work
        keys = pl.ds(pl.multiple_of(base + ch * part, 32), part)
        ka = jnp.concatenate([kvwin[0, keys, :], ohk[keys, :]], axis=1)
        s = dot(ka, qa, NT)
        if ch == 2:
            tail = s[part - PAIR :]
            key_at = lax.broadcasted_iota(jnp.int32, (PAIR, COLS), 0) * QPK
            col_at = lax.broadcasted_iota(jnp.int32, (PAIR, COLS), 1)
            tail = jnp.where(key_at <= col_at, tail, -BIG)
            s = jnp.concatenate([s[: part - PAIR], tail], axis=0)
        s_ref[buf, ch * part : (ch + 1) * part, :] = s
        return jnp.max(s.reshape(part // 8, 8, COLS), axis=0)

    def top(parts):
        return jnp.max(functools.reduce(jnp.maximum, parts), axis=0, keepdims=True)

    def exponentials(work, buf, m, chunks):
        total = jnp.zeros((8, COLS), F32)
        for ch in chunks:
            at = slice(ch * PAIR, (ch + 1) * PAIR)
            e = jnp.exp2((s_ref[buf, at, :] - m) * (SCALE * LOG2E))
            total = total + jnp.sum(e.reshape(PAIR // 8, 8, COLS), axis=0)
            p_all[work[0], at, :] = e.astype(BF16)
        return total

    def weigh(work, total):
        jj, _, qf, _ = work
        rl = 1.0 / jnp.sum(total, axis=0, keepdims=True)
        rls[jj] = rl
        by_row = jnp.broadcast_to(rl, (DIM, COLS)).T
        rowl[jj] = by_row
        qm[jj] = (qf * by_row).astype(BF16)
        return rl

    def attend(work, rl):
        jj, base, _, _ = work
        ot = dot(kvwin[1, pl.ds(base, BAND), :], p_all[jj], TN) * rl
        ot = ot.astype(BF16).astype(F32)
        oall[jj] = ot
        att_ref[pl.ds(base, PAIR)] = ot.T.reshape(PAIR, QPK, DIM).astype(BF16)

    def forward(h, carry):
        one, two_ = load_pair(2 * h), load_pair(2 * h + 1)
        m_one = top([scores(one, 0, ch) for ch in range(3)])

        @pl.when(h == 0)
        def _():
            for d in (1, 3):
                block_arrived(1, d)

        tops, total = [], 0.0
        for ch, chunks in enumerate((range(5), range(5, 9), range(9, 13))):
            tops.append(scores(two_, 1, ch))
            total = total + exponentials(one, 0, m_one, chunks)
        rl_one = weigh(one, total)
        m_two = top(tops)
        attend(one, rl_one)
        total = exponentials(two_, 1, m_two, range(13))
        attend(two_, weigh(two_, total))
        return carry

    lax.fori_loop(0, PAIRS // 2, forward, 0)

    def take_grad(t, carry):
        jj, base = pair(t)
        pair_arrived(3, dobuf, jj, base)
        dof = dobuf[pl.ds(base, PAIR)].astype(F32).reshape(COLS, DIM)
        dom[jj] = dof.astype(BF16)
        doms[jj] = (dof * rowl[jj]).astype(BF16)
        delta[jj] = jnp.sum(dof.T * oall[jj], axis=0, keepdims=True)
        return carry

    lax.fori_loop(0, PAIRS, take_grad, 0)

    def unit(jj, lo, size, off, first=False):
        keys = pl.ds(lo, size)
        ks = kvwin[0, keys, :]
        p = p_all[jj, pl.ds(off, size), :]
        dpt = dot(kvwin[1, keys, :], dom[jj], NT)
        ds = p * (dpt - delta[jj]).astype(BF16)
        dv_acc[keys, :] += dot(p, doms[jj], NN)
        dk_acc[keys, :] += dot(ds, qm[jj], NN)
        if first:
            dqt[jj] = dot(ks, ds, TN)
        else:
            dqt[jj] += dot(ks, ds, TN)

    def put_dq(jj, carry):
        dq = (dqt[jj] * (rls[jj] * SCALE)).T
        rows = pl.ds(pl.multiple_of(jj * PAIR, PAIR), PAIR)
        dq_ref[rows] = dq.reshape(PAIR, QPK, DIM).astype(BF16)
        return carry

    def grad_copy(d):
        return pltpu.make_async_remote_copy(
            src_ref=gsend.at[d - 1], dst_ref=grecv.at[d - 1],
            send_sem=g_send.at[d - 1], recv_sem=g_recv.at[d - 1],
            device_id=((sibling, c - 2, c - 1)[d - 1], g), device_id_type=MESH,
        )

    odd_f = odd.astype(F32)
    sends = ((odd == 1) | before(2), before(2), before(3))
    takes = ((odd == 0) | before(3), behind(2), behind(1) & before(2))

    def grad_arrived(d):
        @pl.when(takes[d - 1])
        def _():
            arrived(grecv.at[d - 1], g_recv.at[d - 1])

        @pl.when(jnp.logical_not(takes[d - 1]))
        def _():
            grecv[d - 1] = jnp.zeros((2, ROWS, DIM), BF16)

    def terms(d):
        rows = slice(own - d * ROWS, own - d * ROWS + ROWS)
        return dk_acc[rows, :] * SCALE, dv_acc[rows, :]

    def send_terms(d, with_sibling=False):
        dk, dv = terms(d)
        if d == 2:
            grad_arrived(3)
            dk = dk + grecv[2, 0].astype(F32)
            dv = dv + grecv[2, 1].astype(F32)
        if with_sibling:
            dk = dk + grecv[0, 0].astype(F32)
            dv = dv + grecv[0, 1].astype(F32)
        gsend[d - 1, 0] = dk.astype(BF16)
        gsend[d - 1, 1] = dv.astype(BF16)

        @pl.when(sends[d - 1])
        def _():
            grad_copy(d).start()

    def whole_block(d):
        lo = pl.multiple_of(own - d * ROWS, ROWS)

        def step(jj, carry):
            unit(jj, lo, ROWS, pl.multiple_of(lo - jj * PAIR, PAIR))
            return carry

        lax.fori_loop(0, PAIRS, step, 0)

    for jj in range(PAIRS):
        unit(jj, jj * PAIR, ROWS - jj * PAIR, 0, first=True)
    send_terms(3)
    whole_block(1 + odd)

    @pl.when(odd == 0)
    def _():
        send_terms(1)

    @pl.when(odd == 1)
    def _():
        grad_arrived(1)
        send_terms(2, with_sibling=True)

    whole_block(2 - odd)

    @pl.when(odd == 0)
    def _():
        send_terms(2)

    @pl.when(odd == 1)
    def _():
        send_terms(1)

    for jj in range(PAIRS):
        unit(jj, own, (jj + 1) * PAIR, own - jj * PAIR)

    lax.fori_loop(0, PAIRS, put_dq, 0)

    dk, dv = terms(0)

    @pl.when(odd == 0)
    def _():
        grad_arrived(1)

    dk = dk + (1.0 - odd_f) * grecv[0, 0].astype(F32)
    dv = dv + (1.0 - odd_f) * grecv[0, 1].astype(F32)
    grad_arrived(2)
    dk_ref[...] = (dk + grecv[1, 0].astype(F32)).astype(BF16)
    dv_ref[...] = (dv + grecv[1, 1].astype(F32)).astype(BF16)

    for slot, peer in enumerate(peers):
        for i in range(2):
            kv_copy(i, peer, slot).wait_send()
            wide_copy(2 + i, *wide[i], peer, slot).wait_send()
    for i in range(2):
        for copy, sent in (
            (to_two(i), two), (to_sibling(i, 0), even_sibling | odd_sibling), (to_three(i), three)
        ):
            @pl.when(sent)
            def _():
                copy.wait_send()
    for d in range(1, SPAN + 1):
        @pl.when(sends[d - 1])
        def _():
            grad_copy(d).wait_send()
    if greet:
        for n, where in ((0, relay_on), (1, relay_on & (odd == 1))):
            @pl.when(where)
            def _():
                from_relay(n).wait_send()


def put_out(*refs):
    sems = refs[-1]
    n = (len(refs) - 1) // 2
    copies = [pltpu.make_async_copy(refs[i], refs[n + i], sems.at[i]) for i in range(n)]
    for copy in copies:
        copy.start()
    for copy in copies:
        copy.wait()


def local(n_ctx, queries, keys, values, grad_out, segment_ids):
    vmem = pl.BlockSpec(memory_space=pltpu.VMEM)
    anywhere = pl.BlockSpec(memory_space=pl.ANY)
    shapes = ((ROWS, QPK, DIM), (ROWS, QPK, DIM), (ROWS, DIM), (ROWS, DIM))
    results = pl.pallas_call(
        functools.partial(kernel, n_ctx),
        out_shape=tuple(pltpu.VMEM(shape, BF16) for shape in shapes),
        in_specs=[anywhere, anywhere, vmem, vmem, vmem],
        out_specs=(vmem,) * 4,
        scratch_shapes=[
            pltpu.VMEM((PIECE * GROUPS, DIM), F32),
            pltpu.VMEM((GROUPS, 2, PIECE, DIM), BF16),
            pltpu.VMEM((2, WINDOW, DIM), BF16),
            pltpu.VMEM((WINDOW, DIM), BF16),
            pltpu.VMEM((ROWS, DIM), F32),
            pltpu.VMEM((ROWS, QPK, DIM), BF16),
            pltpu.VMEM((ROWS, QPK, DIM), BF16),
            pltpu.VMEM((PAIRS, COLS, DIM), BF16),
            pltpu.VMEM((PAIRS, COLS, DIM), BF16),
            pltpu.VMEM((PAIRS, COLS, DIM), BF16),
            pltpu.VMEM((2, BAND, COLS), F32),
            pltpu.VMEM((PAIRS, BAND, COLS), BF16),
            pltpu.VMEM((PAIRS, 1, COLS), F32),
            pltpu.VMEM((PAIRS, 1, COLS), F32),
            pltpu.VMEM((PAIRS, COLS, DIM), F32),
            pltpu.VMEM((PAIRS, DIM, COLS), F32),
            pltpu.VMEM((PAIRS, DIM, COLS), F32),
            pltpu.VMEM((WINDOW, DIM), F32),
            pltpu.VMEM((WINDOW, DIM), F32),
            pltpu.VMEM((SPAN, 2, ROWS, DIM), BF16),
            pltpu.VMEM((SPAN, 2, ROWS, DIM), BF16),
            pltpu.VMEM((2, ROWS, DIM), BF16),
            pltpu.SemaphoreType.DMA((4, GROUPS - 1)),
            pltpu.SemaphoreType.DMA((4, GROUPS)),
            pltpu.SemaphoreType.DMA((2,)),
            pltpu.SemaphoreType.DMA((2,)),
            pltpu.SemaphoreType.DMA((2, SPAN)),
            pltpu.SemaphoreType.DMA((2, SPAN)),
            pltpu.SemaphoreType.DMA((SPAN,)),
            pltpu.SemaphoreType.DMA((SPAN,)),
        ],
        compiler_params=pltpu.CompilerParams(
            collective_id=0, has_side_effects=True, vmem_limit_bytes=56 << 20
        ),
        cost_estimate=pl.CostEstimate(
            flops=12 * DIM * PAIRS * BAND * COLS,
            bytes_accessed=4 * 2 * ROWS * QPK * DIM,
            transcendentals=PAIRS * BAND * COLS,
        ),
    )(
        queries.reshape(PIECE, GROUPS, QPK, DIM),
        grad_out.reshape(PIECE, GROUPS, QPK, DIM),
        keys,
        values,
        segment_ids.reshape(-1, DIM),
    )
    attention, grad_queries, grad_keys, grad_values = pl.pallas_call(
        put_out,
        out_shape=tuple(jax.ShapeDtypeStruct(shape, BF16) for shape in shapes),
        in_specs=[anywhere] * 4,
        out_specs=(anywhere,) * 4,
        scratch_shapes=[pltpu.SemaphoreType.DMA((4,))],
        compiler_params=pltpu.CompilerParams(vmem_limit_bytes=1 << 20),
    )(*[pltpu.with_memory_space_constraint(r, pltpu.VMEM) for r in results])
    return (
        attention,
        grad_queries,
        grad_keys.reshape(ROWS, 1, DIM),
        grad_values.reshape(ROWS, 1, DIM),
    )


def solution(mesh):
    rows = P(("ctx", "kvh"), None, None)
    heads = P("ctx", "kvh", None)
    return jax.shard_map(
        functools.partial(local, mesh.shape["ctx"]),
        mesh=mesh,
        in_specs=(rows, rows, rows, rows, P()),
        out_specs=(heads, heads, heads, heads),
        check_vma=False,
    )
```

```python
import functools
import math

import jax
import jax.numpy as jnp
from jax import lax
from jax.experimental import pallas as pl
from jax.experimental.pallas import tpu as pltpu
from jax.sharding import PartitionSpec as P

MESH = pl.DeviceIdType.MESH
SPAN = 3
GROUP = 16
BIG = 1e30
F32 = jnp.float32
BF16 = jnp.bfloat16

ROWS = 384
PIECE = 48
GROUPS = 8
QPK = 8
DIM = 128
PAIR = 2 * PIECE
PAIRS = ROWS // PAIR
COLS = PAIR * QPK
WINDOW = (SPAN + 1) * ROWS
BAND = SPAN * ROWS + PAIR
SCALE = 1.0 / math.sqrt(DIM)
LOG2E = math.log2(math.e)

NT = (((1,), (1,)), ((), ()))
TN = (((0,), (0,)), ((), ()))
NN = (((1,), (0,)), ((), ()))


def dot(a, b, dims):
    return lax.dot_general(a, b, dims, preferred_element_type=F32)


def kernel(
    n_ctx,
    q_ref, do_ref, k_ref, v_ref, seg_ref,
    att_ref, dq_ref, dk_ref, dv_ref,
    stage, kvsend, kvwin, ohk, ohq, qbuf, dobuf, qm, dom, doms, s_ref, p_all, delta, rls,
    rowl, oall, dqt, dk_acc, dv_acc, gsend, grecv, rbuf,
    a2a_send, a2a_recv, rel_send, rel_recv, fwd_send, fwd_recv, g_send, g_recv,
):
    c = lax.axis_index("ctx")
    g = lax.axis_index("kvh")
    x = g // 2
    odd = lax.rem(c, 2)
    sibling = c + 1 - 2 * odd

    barrier = pltpu.get_barrier_semaphore()
    for s in range(1, GROUPS):
        pl.semaphore_signal(
            barrier, inc=1, device_id=(c, lax.rem(g + s, GROUPS)), device_id_type=MESH
        )

    def before(d):
        return c >= d

    def behind(d):
        return c + d < n_ctx

    for d in (1, 2):
        for there, exists in ((c + d, behind(d)), (c - d, before(d))):
            @pl.when(exists)
            def _():
                pl.semaphore_signal(barrier, inc=1, device_id=(there, g), device_id_type=MESH)

    place = lax.rem(c, GROUP)
    first_y, last_y = place < 2, place >= GROUP - 2
    over_on = last_y & behind(2)
    relay_on = last_y & before(GROUP)
    greet = (
        (c + GROUP, over_on),
        (c - GROUP, relay_on),
        (c + GROUP - 2, first_y & before(GROUP)),
        (c - GROUP + 2, relay_on),
        (c + GROUP - 1, first_y & (odd == 0) & before(GROUP)),
        (c - GROUP + 1, relay_on & (odd == 1)),
    )
    greet = greet if n_ctx > GROUP else ()
    for there, exists in greet:
        @pl.when(exists)
        def _():
            pl.semaphore_signal(barrier, inc=1, device_id=(there, g), device_id_type=MESH)

    for i, ref in enumerate((k_ref, v_ref)):
        stage[...] = ref[...].astype(F32).reshape(PIECE * GROUPS, DIM)
        for h in range(GROUPS):
            kvsend[h, i] = stage[pl.ds(h, PIECE, stride=GROUPS), :].astype(BF16)

    partners = sum(e(d).astype(jnp.int32) for e in (before, behind) for d in (1, 2))
    partners = partners + sum(exists.astype(jnp.int32) for _, exists in greet)
    pl.semaphore_wait(barrier, partners + (GROUPS - 1))

    own = SPAN * ROWS
    my_rows = pl.ds(pl.multiple_of(g * PIECE, PIECE), PIECE)

    def kv_slot(i):
        return kvwin.at[i, pl.ds(pl.multiple_of(own + g * PIECE, PIECE), PIECE)]

    def kv_copy(i, peer, slot):
        return pltpu.make_async_remote_copy(
            src_ref=kvsend.at[peer, i], dst_ref=kv_slot(i),
            send_sem=a2a_send.at[i, slot], recv_sem=a2a_recv.at[i, g],
            device_id=(c, peer), device_id_type=MESH,
        )

    def wide_copy(i, src, dst, peer, slot):
        return pltpu.make_async_remote_copy(
            src_ref=src.at[:, peer], dst_ref=dst.at[my_rows],
            send_sem=a2a_send.at[i, slot], recv_sem=a2a_recv.at[i, g],
            device_id=(c, peer), device_id_type=MESH,
        )

    peers = []
    z = lax.rem(g, 2)
    for step in (0, 1, 3, 2):
        px = lax.rem(x + step, PAIRS)
        for other in (0, 1):
            if step == 0 and other == 0:
                continue
            peers.append(2 * px + lax.rem(z + other, 2))

    wide = ((q_ref, qbuf), (do_ref, dobuf))

    def send_wide(i, slots):
        for slot in slots:
            wide_copy(i, *wide[i - 2], peers[slot], slot).start()

    def arrived(ref, sem):
        pltpu.make_async_copy(ref, ref, sem).wait()

    for i in range(2):
        for slot, peer in enumerate(peers):
            kv_copy(i, peer, slot).start()
        pltpu.make_async_copy(kvsend.at[g, i], kv_slot(i), a2a_recv.at[i, g]).start()
    send_wide(2, (0, 1, 3))
    pltpu.make_async_copy(q_ref.at[:, g], qbuf.at[my_rows], a2a_recv.at[2, g]).start()
    pltpu.make_async_copy(do_ref.at[:, g], dobuf.at[my_rows], a2a_recv.at[3, g]).start()

    def block(i, d):
        return kvwin.at[i, pl.ds(own - d * ROWS, ROWS)]

    def fwd_copy(i, n, src, d, there):
        return pltpu.make_async_remote_copy(
            src_ref=src, dst_ref=block(i, d),
            send_sem=fwd_send.at[i, n], recv_sem=fwd_recv.at[i, d - 1],
            device_id=(there, g), device_id_type=MESH,
        )

    def to_two(i):
        return fwd_copy(i, 0, block(i, 0), 2, c + 2)

    def to_sibling(i, d):
        return fwd_copy(i, 1, block(i, d), 1, sibling)

    def to_three(i):
        return fwd_copy(i, 2, block(i, 2), 3, c + 1)

    def to_relay(n):
        return pltpu.make_async_remote_copy(
            src_ref=block(0, 2 * n), dst_ref=rbuf.at[n],
            send_sem=fwd_send.at[0, 2 * n], recv_sem=rel_recv.at[n],
            device_id=(c + GROUP, g), device_id_type=MESH,
        )

    def from_relay(n):
        return pltpu.make_async_remote_copy(
            src_ref=rbuf.at[n], dst_ref=block(0, 2 + n),
            send_sem=rel_send.at[n], recv_sem=fwd_recv.at[0, 1 + n],
            device_id=(c - GROUP + 2 - n, g), device_id_type=MESH,
        )

    def start_on(i, n, plain, valid):
        if i == 0 and greet:
            @pl.when(valid & over_on)
            def _():
                to_relay(n).start()

            valid = valid & jnp.logical_not(over_on)

        @pl.when(valid)
        def _():
            plain(i).start()

    two = behind(2)
    three = before(2) & behind(1)
    even_sibling = odd == 0
    odd_sibling = (odd == 1) & before(2)

    for i in range(2):
        for j in range(GROUPS):
            arrived(kvwin.at[i, pl.ds(own + j * PIECE, PIECE)], a2a_recv.at[i, j])

        start_on(i, 0, to_two, two)

        @pl.when(even_sibling)
        def _():
            to_sibling(i, 0).start()

    send_wide(2, (2, 4, 5, 6))

    tiles = WINDOW // DIM
    seg_rows = n_ctx * ROWS // DIM
    first = c * (ROWS // DIM) + seg_rows - SPAN * (ROWS // DIM)
    number = lax.broadcasted_iota(jnp.int32, (DIM, DIM), 0)
    for i in range(tiles):
        row = seg_ref[pl.ds(lax.rem(first + i, seg_rows), 1), :]
        hot = jnp.where(number == row, 1.0, 0.0).T
        ohk[i * DIM : (i + 1) * DIM, :] = hot.astype(BF16)
        if i >= tiles - ROWS // DIM:
            at = (i - (tiles - ROWS // DIM)) * DIM
            ohq[at : at + DIM, :] = (hot - 1.0) * BIG
    dk_acc[...] = jnp.zeros_like(dk_acc)
    dv_acc[...] = jnp.zeros_like(dv_acc)

    for d in (1, 2, 3):
        @pl.when(jnp.logical_not(before(d)))
        def _():
            kvwin[:, own - d * ROWS : own - (d - 1) * ROWS, :] = jnp.zeros((2, ROWS, DIM), BF16)

    def block_arrived(i, d):
        @pl.when(before(d))
        def _():
            arrived(block(i, d), fwd_recv.at[i, d - 1])

    for i in range(2):
        block_arrived(i, 2)

        if i == 0 and greet:
            start_on(0, 1, to_three, three & (odd == 1))

            @pl.when(three & (odd == 0))
            def _():
                to_three(0).start()
        else:
            start_on(i, 1, to_three, three)

        @pl.when(odd_sibling)
        def _():
            to_sibling(i, 2).start()

    if greet:
        for n, where in ((0, relay_on), (1, relay_on & (odd == 1))):
            @pl.when(where)
            def _():
                arrived(rbuf.at[n], rel_recv.at[n])
                from_relay(n).start()

    send_wide(3, range(GROUPS - 1))

    for d in (1, 3):
        block_arrived(0, d)

    def pair(t):
        step = jnp.where(t == 0, 0, jnp.where(t == 1, 3, jnp.where(t == 2, 1, 2)))
        jj = lax.rem(x + step, PAIRS)
        return jj, pl.multiple_of(jj * PAIR, PAIR)

    def pair_arrived(i, buf, jj, base):
        for half in range(2):
            piece = pl.ds(pl.multiple_of(base + half * PIECE, PIECE), PIECE)
            arrived(buf.at[piece], a2a_recv.at[i, 2 * jj + half])

    part = BAND // 3

    def load_pair(t):
        jj, base = pair(t)
        rows = pl.ds(base, PAIR)
        pair_arrived(2, qbuf, jj, base)
        qf = qbuf[rows].astype(F32).reshape(COLS, DIM)
        penalty = jnp.broadcast_to(ohq[rows, :][:, None, :], (PAIR, QPK, DIM))
        penalty = penalty.reshape(COLS, DIM).astype(BF16)
        return jj, base, qf, jnp.concatenate([qf.astype(BF16), penalty], axis=1)

    def scores(work, buf, ch):
        _, base, _, qa = work
        keys = pl.ds(pl.multiple_of(base + ch * part, 32), part)
        ka = jnp.concatenate([kvwin[0, keys, :], ohk[keys, :]], axis=1)
        s = dot(ka, qa, NT)
        if ch == 2:
            tail = s[part - PAIR :]
            key_at = lax.broadcasted_iota(jnp.int32, (PAIR, COLS), 0) * QPK
            col_at = lax.broadcasted_iota(jnp.int32, (PAIR, COLS), 1)
            tail = jnp.where(key_at <= col_at, tail, -BIG)
            s = jnp.concatenate([s[: part - PAIR], tail], axis=0)
        s_ref[buf, ch * part : (ch + 1) * part, :] = s
        return jnp.max(s.reshape(part // 8, 8, COLS), axis=0)

    def top(parts):
        return jnp.max(functools.reduce(jnp.maximum, parts), axis=0, keepdims=True)

    def exponentials(work, buf, m, chunks):
        total = jnp.zeros((8, COLS), F32)
        for ch in chunks:
            at = slice(ch * PAIR, (ch + 1) * PAIR)
            e = jnp.exp2((s_ref[buf, at, :] - m) * (SCALE * LOG2E))
            total = total + jnp.sum(e.reshape(PAIR // 8, 8, COLS), axis=0)
            p_all[work[0], at, :] = e.astype(BF16)
        return total

    def weigh(work, total):
        jj, _, qf, _ = work
        rl = 1.0 / jnp.sum(total, axis=0, keepdims=True)
        rls[jj] = rl
        by_row = jnp.broadcast_to(rl, (DIM, COLS)).T
        rowl[jj] = by_row
        qm[jj] = (qf * by_row).astype(BF16)
        return rl

    def attend(work, rl):
        jj, base, _, _ = work
        ot = dot(kvwin[1, pl.ds(base, BAND), :], p_all[jj], TN) * rl
        ot = ot.astype(BF16).astype(F32)
        oall[jj] = ot
        att_ref[pl.ds(base, PAIR)] = ot.T.reshape(PAIR, QPK, DIM).astype(BF16)

    def forward(h, carry):
        one, two_ = load_pair(2 * h), load_pair(2 * h + 1)
        m_one = top([scores(one, 0, ch) for ch in range(3)])

        @pl.when(h == 0)
        def _():
            for d in (1, 3):
                block_arrived(1, d)

        tops, total = [], 0.0
        for ch, chunks in enumerate((range(5), range(5, 9), range(9, 13))):
            tops.append(scores(two_, 1, ch))
            total = total + exponentials(one, 0, m_one, chunks)
        rl_one = weigh(one, total)
        m_two = top(tops)
        attend(one, rl_one)
        total = exponentials(two_, 1, m_two, range(13))
        attend(two_, weigh(two_, total))
        return carry

    lax.fori_loop(0, PAIRS // 2, forward, 0)

    def take_grad(t, carry):
        jj, base = pair(t)
        pair_arrived(3, dobuf, jj, base)
        dof = dobuf[pl.ds(base, PAIR)].astype(F32).reshape(COLS, DIM)
        dom[jj] = dof.astype(BF16)
        doms[jj] = (dof * rowl[jj]).astype(BF16)
        delta[jj] = jnp.sum(dof.T * oall[jj], axis=0, keepdims=True)
        dqt[jj] = jnp.zeros((DIM, COLS), F32)
        return carry

    def unit(jj, lo, size, off):
        keys = pl.ds(lo, size)
        ks = kvwin[0, keys, :]
        p = p_all[jj, pl.ds(off, size), :]
        dpt = dot(kvwin[1, keys, :], dom[jj], NT)
        ds = p * (dpt - delta[jj]).astype(BF16)
        dv_acc[keys, :] += dot(p, doms[jj], NN)
        dk_acc[keys, :] += dot(ds, qm[jj], NN)
        dqt[jj] += dot(ks, ds, TN)

    def put_dq(t, carry):
        jj, _ = pair(t)
        dq = (dqt[jj] * (rls[jj] * SCALE)).T
        rows = pl.ds(pl.multiple_of(jj * PAIR, PAIR), PAIR)
        dq_ref[rows] = dq.reshape(PAIR, QPK, DIM).astype(BF16)
        return carry

    early = PAIRS // 2

    def backward(t, carry):
        take_grad(t, 0)
        jj, base = pair(t)
        for ch in range(3):
            unit(jj, pl.multiple_of(base + ch * part, 32), part, ch * part)
        return put_dq(t, carry)

    lax.fori_loop(0, early, backward, 0)
    lax.fori_loop(early, PAIRS, take_grad, 0)

    def grad_copy(d):
        return pltpu.make_async_remote_copy(
            src_ref=gsend.at[d - 1], dst_ref=grecv.at[d - 1],
            send_sem=g_send.at[d - 1], recv_sem=g_recv.at[d - 1],
            device_id=((sibling, c - 2, c - 1)[d - 1], g), device_id_type=MESH,
        )

    odd_f = odd.astype(F32)
    sends = ((odd == 1) | before(2), before(2), before(3))
    takes = ((odd == 0) | before(3), behind(2), behind(1) & before(2))

    def grad_arrived(d):
        @pl.when(takes[d - 1])
        def _():
            arrived(grecv.at[d - 1], g_recv.at[d - 1])

        @pl.when(jnp.logical_not(takes[d - 1]))
        def _():
            grecv[d - 1] = jnp.zeros((2, ROWS, DIM), BF16)

    def terms(d):
        rows = slice(own - d * ROWS, own - d * ROWS + ROWS)
        return dk_acc[rows, :] * SCALE, dv_acc[rows, :]

    def send_terms(d, with_sibling=False):
        dk, dv = terms(d)
        if d == 2:
            grad_arrived(3)
            dk = dk + grecv[2, 0].astype(F32)
            dv = dv + grecv[2, 1].astype(F32)
        if with_sibling:
            dk = dk + grecv[0, 0].astype(F32)
            dv = dv + grecv[0, 1].astype(F32)
        gsend[d - 1, 0] = dk.astype(BF16)
        gsend[d - 1, 1] = dv.astype(BF16)

        @pl.when(sends[d - 1])
        def _():
            grad_copy(d).start()

    def whole_block(d):
        lo = pl.multiple_of(own - d * ROWS, ROWS)

        def step(t, carry):
            jj, _ = pair(t)
            unit(jj, lo, ROWS, pl.multiple_of(lo - jj * PAIR, PAIR))
            return carry

        lax.fori_loop(early, PAIRS, step, 0)

    def end_block(far):
        def step(t, carry):
            jj, _ = pair(t)
            for v in range(PAIRS):
                @pl.when(jj == v)
                def _():
                    if far:
                        unit(v, v * PAIR, ROWS - v * PAIR, 0)
                    else:
                        unit(v, own, (v + 1) * PAIR, own - v * PAIR)
            return carry

        lax.fori_loop(early, PAIRS, step, 0)

    end_block(True)
    send_terms(3)
    whole_block(1 + odd)

    @pl.when(odd == 0)
    def _():
        send_terms(1)

    @pl.when(odd == 1)
    def _():
        grad_arrived(1)
        send_terms(2, with_sibling=True)

    whole_block(2 - odd)

    @pl.when(odd == 0)
    def _():
        send_terms(2)

    @pl.when(odd == 1)
    def _():
        send_terms(1)

    end_block(False)
    lax.fori_loop(early, PAIRS, put_dq, 0)

    dk, dv = terms(0)

    @pl.when(odd == 0)
    def _():
        grad_arrived(1)

    dk = dk + (1.0 - odd_f) * grecv[0, 0].astype(F32)
    dv = dv + (1.0 - odd_f) * grecv[0, 1].astype(F32)
    grad_arrived(2)
    dk_ref[...] = (dk + grecv[1, 0].astype(F32)).astype(BF16)
    dv_ref[...] = (dv + grecv[1, 1].astype(F32)).astype(BF16)

    for slot, peer in enumerate(peers):
        for i in range(2):
            kv_copy(i, peer, slot).wait_send()
            wide_copy(2 + i, *wide[i], peer, slot).wait_send()
    for i in range(2):
        for copy, sent in (
            (to_two(i), two), (to_sibling(i, 0), even_sibling | odd_sibling), (to_three(i), three)
        ):
            @pl.when(sent)
            def _():
                copy.wait_send()
    for d in range(1, SPAN + 1):
        @pl.when(sends[d - 1])
        def _():
            grad_copy(d).wait_send()
    if greet:
        for n, where in ((0, relay_on), (1, relay_on & (odd == 1))):
            @pl.when(where)
            def _():
                from_relay(n).wait_send()


def put_out(*refs):
    sems = refs[-1]
    n = (len(refs) - 1) // 2
    copies = [pltpu.make_async_copy(refs[i], refs[n + i], sems.at[i]) for i in range(n)]
    for copy in copies:
        copy.start()
    for copy in copies:
        copy.wait()


def local(n_ctx, queries, keys, values, grad_out, segment_ids):
    vmem = pl.BlockSpec(memory_space=pltpu.VMEM)
    anywhere = pl.BlockSpec(memory_space=pl.ANY)
    shapes = ((ROWS, QPK, DIM), (ROWS, QPK, DIM), (ROWS, DIM), (ROWS, DIM))
    results = pl.pallas_call(
        functools.partial(kernel, n_ctx),
        out_shape=tuple(pltpu.VMEM(shape, BF16) for shape in shapes),
        in_specs=[anywhere, anywhere, vmem, vmem, vmem],
        out_specs=(vmem,) * 4,
        scratch_shapes=[
            pltpu.VMEM((PIECE * GROUPS, DIM), F32),
            pltpu.VMEM((GROUPS, 2, PIECE, DIM), BF16),
            pltpu.VMEM((2, WINDOW, DIM), BF16),
            pltpu.VMEM((WINDOW, DIM), BF16),
            pltpu.VMEM((ROWS, DIM), F32),
            pltpu.VMEM((ROWS, QPK, DIM), BF16),
            pltpu.VMEM((ROWS, QPK, DIM), BF16),
            pltpu.VMEM((PAIRS, COLS, DIM), BF16),
            pltpu.VMEM((PAIRS, COLS, DIM), BF16),
            pltpu.VMEM((PAIRS, COLS, DIM), BF16),
            pltpu.VMEM((2, BAND, COLS), F32),
            pltpu.VMEM((PAIRS, BAND, COLS), BF16),
            pltpu.VMEM((PAIRS, 1, COLS), F32),
            pltpu.VMEM((PAIRS, 1, COLS), F32),
            pltpu.VMEM((PAIRS, COLS, DIM), F32),
            pltpu.VMEM((PAIRS, DIM, COLS), F32),
            pltpu.VMEM((PAIRS, DIM, COLS), F32),
            pltpu.VMEM((WINDOW, DIM), F32),
            pltpu.VMEM((WINDOW, DIM), F32),
            pltpu.VMEM((SPAN, 2, ROWS, DIM), BF16),
            pltpu.VMEM((SPAN, 2, ROWS, DIM), BF16),
            pltpu.VMEM((2, ROWS, DIM), BF16),
            pltpu.SemaphoreType.DMA((4, GROUPS - 1)),
            pltpu.SemaphoreType.DMA((4, GROUPS)),
            pltpu.SemaphoreType.DMA((2,)),
            pltpu.SemaphoreType.DMA((2,)),
            pltpu.SemaphoreType.DMA((2, SPAN)),
            pltpu.SemaphoreType.DMA((2, SPAN)),
            pltpu.SemaphoreType.DMA((SPAN,)),
            pltpu.SemaphoreType.DMA((SPAN,)),
        ],
        compiler_params=pltpu.CompilerParams(
            collective_id=0, has_side_effects=True, vmem_limit_bytes=56 << 20
        ),
        cost_estimate=pl.CostEstimate(
            flops=12 * DIM * PAIRS * BAND * COLS,
            bytes_accessed=4 * 2 * ROWS * QPK * DIM,
            transcendentals=PAIRS * BAND * COLS,
        ),
    )(
        queries.reshape(PIECE, GROUPS, QPK, DIM),
        grad_out.reshape(PIECE, GROUPS, QPK, DIM),
        keys,
        values,
        segment_ids.reshape(-1, DIM),
    )
    attention, grad_queries, grad_keys, grad_values = pl.pallas_call(
        put_out,
        out_shape=tuple(jax.ShapeDtypeStruct(shape, BF16) for shape in shapes),
        in_specs=[anywhere] * 4,
        out_specs=(anywhere,) * 4,
        scratch_shapes=[pltpu.SemaphoreType.DMA((4,))],
        compiler_params=pltpu.CompilerParams(vmem_limit_bytes=1 << 20),
    )(*[pltpu.with_memory_space_constraint(r, pltpu.VMEM) for r in results])
    return (
        attention,
        grad_queries,
        grad_keys.reshape(ROWS, 1, DIM),
        grad_values.reshape(ROWS, 1, DIM),
    )


def solution(mesh):
    rows = P(("ctx", "kvh"), None, None)
    heads = P("ctx", "kvh", None)
    return jax.shard_map(
        functools.partial(local, mesh.shape["ctx"]),
        mesh=mesh,
        in_specs=(rows, rows, rows, rows, P()),
        out_specs=(heads, heads, heads, heads),
        check_vma=False,
    )
```
